256 devices in a mesh: dp: 64 (over z, y, core), mp: 4 (over x).
Axes of the slice: x: 4, y: 4, z: 8, core: 2. Of those that a mesh axis runs over, the one named last changes fastest.
Arguments:
- tokens: bfloat16 [65536, 4096], P('dp', 'mp'), may hold values from -6 to 6
- cotangent: bfloat16 [65536, 4096], P('dp', 'mp'), may hold values from -6 to 6
- w_query: bfloat16 [4096, 2048], P('dp', 'mp'), may hold values from -6 to 6
- w_key: bfloat16 [4096, 2048], P('dp', 'mp'), may hold values from -6 to 6
- w_value: bfloat16 [4096, 2048], P('dp', 'mp'), may hold values from -0.09375 to 0.09375
- w_out: bfloat16 [2048, 4096], P('mp', 'dp'), may hold values from -0.125 to 0.125
- gain: float32 [4096], replicated, may hold values from 0.25 to 1.75
- w_router: float32 [4096], replicated, may hold values from -0.09375 to 0.09375
- chosen: int32 [8192], P('dp'), may hold values from 0 to 1023, as said below
- counts: int32 [64], P('dp'), may hold values from 32 to 128, as said below
- doc_start: int32 [65536], P('dp'), may hold values from 0 to 1023, as said below
Outputs:
- block_out: bfloat16 [65536, 4096], P('dp', 'mp')
- token_grad: bfloat16 [65536, 4096], P('dp', 'mp')
- muon_step: float32 [2048, 4096], P('mp', 'dp')
The draws below stay inside these ranges and needn't reach their ends.
Inputs may be any that keep to these rules, and one draw needn't show every extreme that they name: `chosen`: within each sequence the list's entries are distinct; the first counts entries are the live rows in increasing order. Every list contains rows 0 and 1023. `counts`: some sequence has all 128 slots live, and some other sequence has exactly 32. Along a sequence doc_start never decreases from one token to the next and never exceeds the token's own position; no document crosses a sequence boundary: the first token of each sequence starts a document, and so does the last.
All inputs are finite; a program needn't handle non-finite values.
Results may differ from the reference program's by a relative error of at most 0.008.
Values may be sent and summed in bfloat16 or wider, within the bound.
No kernel may reach another device: no remote copies, remote signals or barrier semaphores. Data moves between devices by JAX's collectives and lax.ppermute only.
A program may use at most 128 MiB of HBM per device.

```python
import math
import jax
import jax.numpy as jnp
from jax import lax

D = 4096
HEADS = 16
HD = 128
TOK_DEV = 1024
NS_STEPS = 2
CAP = 128
TOKENS = 65536
N_DP = 64


def route_plan(key):
    count_key, order_key, forced_key, low_key = jax.random.split(key, 4)
    live_totals = jax.random.randint(count_key, (N_DP,), CAP // 4, CAP + 1)
    forced = jax.random.randint(forced_key, (), 0, N_DP)
    lowest = (forced + 1 + jax.random.randint(low_key, (), 0, N_DP - 1)) % N_DP
    live_totals = jnp.where(jnp.arange(N_DP) == forced, CAP, live_totals)
    live_totals = jnp.where(jnp.arange(N_DP) == lowest, CAP // 4, live_totals).astype(jnp.int32)

    def one_list(seq_key, live_total):
        inner = jax.random.permutation(seq_key, TOK_DEV - 2).astype(jnp.int32) + 1
        ends = jnp.array([0, TOK_DEV - 1], jnp.int32)
        candidates = jnp.concatenate([ends, inner[:CAP - 2]])
        candidates = jax.random.permutation(jax.random.fold_in(seq_key, 1), candidates)
        sort_keys = jnp.where(jnp.arange(CAP) < live_total, candidates, candidates + TOK_DEV)
        return (jnp.sort(sort_keys) % TOK_DEV).astype(jnp.int32)
    lists = jax.vmap(one_list)(jax.random.split(order_key, N_DP), live_totals)
    return (live_totals, lists.reshape(-1))


def draw_chosen(key, part):
    return route_plan(key)[1]


def draw_counts(key, part):
    return route_plan(key)[0]


def draw_doc_start(key, part):
    key = jax.random.fold_in(key, 7)
    flags = jax.random.randint(key, (N_DP, TOK_DEV), 0, 96) == 0
    flags = flags.at[:, 0].set(True).at[:, TOK_DEV - 1].set(True)
    places = jnp.broadcast_to(jnp.arange(TOK_DEV, dtype=jnp.int32), (N_DP, TOK_DEV))
    starts = jnp.where(flags, places, 0)
    return jax.lax.cummax(starts, axis=1).reshape(-1).astype(jnp.int32)


def projection_pair(key, top_scale, align):
    query_key, key_key, order_key = jax.random.split(jax.random.fold_in(key, 11), 3)
    base_query = jax.random.truncated_normal(query_key, -6.0, 6.0, (D, HEADS * HD), jnp.float32) * D ** (-0.5)
    base_key = jax.random.truncated_normal(key_key, -6.0, 6.0, (D, HEADS * HD), jnp.float32) * D ** (-0.5)
    ranks = jax.random.permutation(order_key, HEADS).astype(jnp.float32)
    ladder = jnp.exp(jnp.log(top_scale) * ranks / max(HEADS - 1, 1))
    aligned = jnp.where(ranks >= HEADS // 2, align, 0.0)
    head_scale = jnp.repeat(ladder, HD)
    head_align = jnp.repeat(aligned, HD)
    query = base_query * head_scale
    keys = (head_align * base_query + jnp.sqrt(1.0 - head_align * head_align) * base_key) * head_scale
    return (query, keys)


def draw_w_query(key, part):
    return projection_pair(key, 1.0, 0.0)[0].astype(jnp.bfloat16)


def draw_w_key(key, part):
    return projection_pair(key, 1.0, 0.0)[1].astype(jnp.bfloat16)


def block_levels(rng, dims, pieces, smallest, top_value):
    def one(dim, blocks):
        steps = jax.random.uniform(jax.random.fold_in(jax.random.fold_in(rng, 6), dim), (blocks,), jnp.float32, smallest / len(pieces), top_value / len(pieces))
        return jnp.repeat(jnp.exp(steps), dims[dim] // blocks).reshape((-1,) + (1,) * (len(dims) - dim - 1))

    factor_of = one(*pieces[0])
    for cut in pieces[1:]:
        factor_of = factor_of * one(*cut)
    return factor_of


def scatter_about(own_key, extent, deviation, most, cuts=(), kind=jnp.bfloat16):
    values = deviation * jax.random.normal(own_key, extent, jnp.float32)
    if cuts:
        values = values * block_levels(own_key, extent, cuts, -0.22, 0.18)
    return jnp.clip(values, -most, most).astype(kind)


def setup_inputs(seed: int = 0) -> dict:
    seeds = jax.random.split(jax.random.key(seed), 12)
    return {
        "tokens": scatter_about(seeds[0], (TOKENS, D), 1.0, 6.0, ((0, 64), (1, 4))),
        "cotangent": scatter_about(seeds[1], (TOKENS, D), 1.0, 6.0, ((0, 64), (1, 4))),
        "w_query": draw_w_query(jax.random.fold_in(seeds[11], 71), 0),
        "w_key": draw_w_key(jax.random.fold_in(seeds[11], 71), 0),
        "w_value": scatter_about(seeds[4], (D, HEADS * HD), D ** -0.5, 0.09375, ((0, 64), (1, 4))),
        "w_out": scatter_about(seeds[5], (HEADS * HD, D), (HEADS * HD) ** -0.5, 0.125, ((0, 4), (1, 64))),
        "gain": jnp.clip(1.0 + 0.15 * jax.random.normal(seeds[6], (D,), jnp.float32), 0.25, 1.75),
        "w_router": scatter_about(seeds[7], (D,), D ** -0.5, 0.09375, (), jnp.float32),
        "chosen": draw_chosen(jax.random.fold_in(seeds[11], 71), 0),
        "counts": draw_counts(jax.random.fold_in(seeds[11], 71), 0),
        "doc_start": draw_doc_start(jax.random.fold_in(seeds[11], 71), 0),
    }


EPS = 1e-06
COEF_A = 3.4445
COEF_B = -4.775
COEF_C = 2.0315

def attend(rows_in, gain, w_query, w_key, w_value, doc_ids, positions, live_mask):
    rows_wide = rows_in.astype(jnp.float32)
    inv_scale = lax.rsqrt(lax.optimization_barrier(jnp.mean(rows_wide * rows_wide, axis=1, keepdims=True)) + EPS)
    unit_rows = rows_wide * inv_scale
    normed = (unit_rows * gain).astype(jnp.bfloat16)
    length = rows_in.shape[0]
    heads_here = w_query.shape[1] // HD

    def project(weight):
        return jnp.dot(normed, weight, preferred_element_type=jnp.float32).astype(jnp.bfloat16).reshape(length, heads_here, HD)
    query = project(w_query)
    key_rows = project(w_key)
    values = project(w_value)
    scores = jnp.einsum('qhd,khd->hqk', query.astype(jnp.float32), key_rows.astype(jnp.float32)) * HD ** (-0.5)
    allowed = (positions[None, :] <= positions[:, None]) & (doc_ids[None, :] == doc_ids[:, None]) & live_mask[None, :]
    allowed = allowed | jnp.eye(length, dtype=bool)
    scores = jnp.where(allowed[None], scores, -1e+30)
    peak = lax.optimization_barrier(jnp.max(scores, axis=2, keepdims=True))
    expo = jnp.exp(scores - peak)
    probs = expo / lax.optimization_barrier(jnp.sum(expo, axis=2, keepdims=True))
    probs_low = probs.astype(jnp.bfloat16)
    attn = jnp.einsum('hqk,khd->qhd', probs_low.astype(jnp.float32), values.astype(jnp.float32)).astype(jnp.bfloat16)
    return (attn.reshape(length, -1), (unit_rows, inv_scale, query, key_rows, values, probs, probs_low))

def attend_back(d_attn, saved, w_query, w_key, w_value):
    unit_rows, inv_scale, query, key_rows, values, probs, probs_low = saved
    length = d_attn.shape[0]
    d_heads = d_attn.reshape(length, -1, HD).astype(jnp.float32)
    d_probs = jnp.einsum('qhd,khd->hqk', d_heads, values.astype(jnp.float32))
    d_scores = (probs * (d_probs - lax.optimization_barrier(jnp.sum(d_probs * probs, axis=2, keepdims=True))) * HD ** (-0.5)).astype(jnp.bfloat16)
    d_query = jnp.einsum('hqk,khd->qhd', d_scores.astype(jnp.float32), key_rows.astype(jnp.float32)).astype(jnp.bfloat16).reshape(length, -1)
    d_keys = jnp.einsum('hqk,qhd->khd', d_scores.astype(jnp.float32), query.astype(jnp.float32)).astype(jnp.bfloat16).reshape(length, -1)
    d_values = jnp.einsum('hqk,qhd->khd', probs_low.astype(jnp.float32), d_heads).astype(jnp.bfloat16).reshape(length, -1)
    total = jnp.dot(d_query, w_query.T, preferred_element_type=jnp.float32)
    total = total + jnp.dot(d_keys, w_key.T, preferred_element_type=jnp.float32)
    return total + jnp.dot(d_values, w_value.T, preferred_element_type=jnp.float32)

def reference(tokens, cotangent, w_query, w_key, w_value, w_out, gain, w_router, chosen, counts, doc_start):
    seq_rows = tokens.reshape(N_DP, TOK_DEV, D)
    seq_grads = cotangent.reshape(N_DP, TOK_DEV, D)
    seq_picks = chosen.reshape(N_DP, CAP)
    seq_docs = doc_start.reshape(N_DP, TOK_DEV)

    def one_seq(w_grad, inputs):
        rows_all, grad_all, picked, live_total, starts = inputs
        rows_in = rows_all[picked]
        grad_in = grad_all[picked]
        live_mask = jnp.arange(CAP) < live_total
        doc_ids = starts[picked]
        attn, saved = attend(rows_in, gain, w_query, w_key, w_value, doc_ids, picked, live_mask)
        mixed = jnp.dot(attn, w_out, preferred_element_type=jnp.float32)
        rows_wide = rows_in.astype(jnp.float32)
        gate_prob = jax.nn.sigmoid(lax.optimization_barrier(jnp.sum(rows_wide * w_router, axis=1)))
        updated = (rows_wide + gate_prob[:, None] * mixed).astype(jnp.bfloat16)
        out_seq = rows_all.at[picked].set(jnp.where(live_mask[:, None], updated, rows_in))
        grad_wide = grad_in.astype(jnp.float32)
        d_mix = (jnp.where(live_mask, gate_prob, 0.0)[:, None] * grad_wide).astype(jnp.bfloat16)
        d_logit = lax.optimization_barrier(jnp.sum(grad_wide * mixed, axis=1)) * gate_prob * (1.0 - gate_prob)
        d_attn = jnp.dot(d_mix, w_out.T, preferred_element_type=jnp.float32).astype(jnp.bfloat16)
        d_normed = attend_back(d_attn, saved, w_query, w_key, w_value)
        unit_rows, inv_scale = (saved[0], saved[1])
        scaled = d_normed * gain
        stat = lax.optimization_barrier(jnp.sum(scaled * unit_rows, axis=1, keepdims=True)) / D
        d_rows = grad_wide + inv_scale * (scaled - unit_rows * stat) + d_logit[:, None] * w_router
        grad_seq = grad_all.at[picked].set(jnp.where(live_mask[:, None], d_rows.astype(jnp.bfloat16), grad_in))
        w_grad = w_grad + jnp.dot(attn.T, d_mix, preferred_element_type=jnp.float32)
        return (w_grad, (out_seq, grad_seq))
    start_grad = jnp.zeros((HEADS * HD, D), jnp.float32)
    w_grad, (out_all, grad_all) = lax.scan(one_seq, start_grad, (seq_rows, seq_grads, seq_picks, counts, seq_docs))
    head_grad = w_grad.reshape(HEADS, HD, D)
    norms = jnp.sqrt(lax.optimization_barrier(jnp.sum(head_grad * head_grad, axis=(1, 2))))
    ortho = head_grad / (norms[:, None, None] + 1e-07)
    for sweep in range(NS_STEPS):
        gram = jnp.einsum('hid,hjd->hij', ortho, ortho, precision=lax.Precision.HIGHEST)
        poly = COEF_B * gram + COEF_C * jnp.einsum('hij,hjk->hik', gram, gram, precision=lax.Precision.HIGHEST)
        ortho = COEF_A * ortho + jnp.einsum('hij,hjd->hid', poly, ortho, precision=lax.Precision.HIGHEST)
    muon_step = (0.2 * math.sqrt(D) * ortho).reshape(HEADS * HD, D)
    return (out_all.reshape(TOKENS, D), grad_all.reshape(TOKENS, D), muon_step)
```

```python
import math

import jax
import jax.numpy as jnp
from jax import lax
from jax.sharding import PartitionSpec as P

D = 4096
HD = 128
NZ, NY, NC, NX = 8, 4, 2, 4
EPS = 1e-06
COEF_A = 3.4445
COEF_B = -4.775
COEF_C = 2.0315
BF = jnp.bfloat16
F32 = jnp.float32


def dp_index(z, y, c):
    return ((z % NZ) * NY + (y % NY)) * NC + c


def dp_perm(dz, dy, dc):
    return [
        (dp_index(z, y, c), dp_index(z + dz, y + dy, (c + dc) % NC))
        for z in range(NZ)
        for y in range(NY)
        for c in range(NC)
    ]


def move_z(v, k):
    return lax.ppermute(v, "dp", dp_perm(k, 0, 0))


def move_y(v, k):
    return lax.ppermute(v, "dp", dp_perm(0, k, 0))


def swap_core(v):
    return lax.ppermute(v, "dp", dp_perm(0, 0, 1))


def move_x(v, k):
    return lax.ppermute(v, "mp", [(i, (i + k) % NX) for i in range(NX)])


def pick(v, i, n):
    return lax.dynamic_index_in_dim(v, lax.rem(i, n), 0, keepdims=False)


def place(buf, v, i, n, *rest):
    start = (lax.rem(i, n),) + rest
    v = v.reshape((1,) * (buf.ndim - v.ndim) + v.shape)
    start = start + (0,) * (buf.ndim - len(start))
    return lax.dynamic_update_slice(buf, v, start)


def ring4(v, move, me, buf):
    half = v.shape[0] // 2
    left = move(v, 1)
    right = move(v, -1)
    far_a = move(left[:half], 1)
    far_b = move(right[half:], -1)
    buf = place(buf, v, me, 4)
    buf = place(buf, left, me + 3, 4)
    buf = place(buf, right, me + 1, 4)
    buf = place(buf, jnp.concatenate([far_a, far_b], axis=0), me + 2, 4)
    return buf


def ring8_parts(v, move):
    half = v.shape[0] // 2
    out = [(0, v)]
    up, down = v, v
    for k in range(1, 4):
        up = move(up, 1)
        down = move(down, -1)
        out += [(8 - k, up), (k, down)]
    far_a = move(up[:half], 1)
    far_b = move(down[half:], -1)
    out.append((4, jnp.concatenate([far_a, far_b], axis=0)))
    return out


def gather_yz(shard, z, y):
    n = shard.shape[1]
    plane = ring4(shard, move_y, y, jnp.zeros((NY, 128, n), BF))
    buf = jnp.zeros((NZ, NY, 128, n), BF)
    for k, block in ring8_parts(plane, move_z):
        buf = place(buf, block, z + k, NZ)
    return buf


def gather_zy(shard, z, y):
    n = shard.shape[1]
    parts = ring8_parts(shard, move_z)
    buf = jnp.zeros((NY, NZ, 128, n), BF)
    for group in (parts[:5], parts[5:]):
        v = jnp.stack([b for _, b in group])
        half = v.shape[0] // 2
        left = move_y(v, 1)
        right = move_y(v, -1)
        far_a = move_y(left[:half], 1)
        far_b = move_y(right[half:], -1)
        far = jnp.concatenate([far_a, far_b], axis=0)
        for dy, block in ((0, v), (3, left), (1, right), (2, far)):
            for j, (k, _) in enumerate(group):
                buf = place(buf, block[j], y + dy, NY, lax.rem(z + k, NZ))
    return buf


def reduce_ring8(g, me):
    half = g.shape[1] // 2
    far = pick(g, me + 4, 8).astype(BF)
    up = move_z(far[:half], 1)
    down = move_z(far[half:], -1)
    own_up = pick(g, me + 3, 8)
    own_down = pick(g, me + 5, 8)
    up = jnp.concatenate([own_up[:half] + up.astype(F32), own_up[half:]], axis=0)
    down = jnp.concatenate([own_down[:half], own_down[half:] + down.astype(F32)], axis=0)
    for k in (2, 1):
        up = move_z(up.astype(BF), 1).astype(F32) + pick(g, me + k, 8)
        down = move_z(down.astype(BF), -1).astype(F32) + pick(g, me + 8 - k, 8)
    up = move_z(up.astype(BF), 1).astype(F32)
    down = move_z(down.astype(BF), -1).astype(F32)
    return up + down + pick(g, me, 8)


def reduce_ring4(g, me, move):
    half = g.shape[1] // 2
    far = pick(g, me + 2, 4).astype(BF)
    up = move(far[:half], 1)
    down = move(far[half:], -1)
    own_up = pick(g, me + 1, 4)
    own_down = pick(g, me + 3, 4)
    up = jnp.concatenate([own_up[:half] + up.astype(F32), own_up[half:]], axis=0)
    down = jnp.concatenate([own_down[:half], own_down[half:] + down.astype(F32)], axis=0)
    up = move(up.astype(BF), 1).astype(F32)
    down = move(down.astype(BF), -1).astype(F32)
    return up + down + pick(g, me, 4)


def gram_total(gram, z):
    gram = gram + (move_y(gram, 1) + move_y(gram, -1)) + move_y(gram, 2)
    parts = gram.reshape(NZ, 32, 128)
    mine = pick(parts, z, NZ)
    for k in range(1, NZ):
        mine = mine + move_z(pick(parts, z + k, NZ), k)
    whole = place(jnp.zeros((NZ, 32, 128), F32), mine, z, NZ)
    for k in range(1, NZ):
        whole = place(whole, move_z(mine, k), z + NZ - k, NZ)
    return whole.reshape(2, 128, 128)


def high_dot(left, right):
    return jnp.einsum("hij,hjk->hik", left, right, precision=lax.Precision.HIGHEST)


def dot_nt(left, right):
    return lax.dot_general(
        left, right, (((1,), (1,)), ((), ())), preferred_element_type=F32
    )


def dot_tn(left, right):
    return lax.dot_general(
        left, right, (((0,), (0,)), ((), ())), preferred_element_type=F32
    )


def per_device(
    tokens, cotangent, w_query, w_key, w_value, w_out, gain, w_router, chosen, counts, doc_start
):
    dp = lax.axis_index("dp")
    x = lax.axis_index("mp")
    c = lax.rem(dp, NC)
    y = lax.rem(lax.div(dp, NC), NY)
    z = lax.div(dp, NC * NY)
    slots = chosen.shape[0]
    feat = tokens.shape[1]

    stacked = jnp.stack([w_query, w_key, w_value, w_out.T]).reshape(4, 64, 2, 256)
    keep = lax.dynamic_index_in_dim(stacked, c, 2, keepdims=False)
    give = lax.dynamic_index_in_dim(stacked, 1 - c, 2, keepdims=False)
    take = swap_core(give)
    first = jnp.where(c == 0, keep, take)
    second = jnp.where(c == 0, take, keep)
    shard = jnp.concatenate([first, second], axis=1).reshape(4, 128, 2, HD)
    shard_a = shard[:, :, 0].transpose(1, 0, 2).reshape(128, 4 * HD)
    shard_b = shard[:, :, 1].transpose(1, 0, 2).reshape(128, 4 * HD)

    picks = chosen[:, None] == jnp.arange(tokens.shape[0])[None, :]
    onehot = picks.astype(BF)
    live_own = jnp.arange(slots) < counts[0]
    docs_own = jnp.sum(jnp.where(picks, doc_start[None, :], 0), axis=1)
    rows_part = jnp.dot(onehot, tokens, preferred_element_type=F32).astype(BF)
    grad_part = jnp.dot(onehot, cotangent, preferred_element_type=F32).astype(BF)
    meta_own = jnp.stack([chosen, docs_own, live_own.astype(jnp.int32)])
    meta = jnp.stack([meta_own, swap_core(meta_own)])

    def all_features(part):
        mine = ring4(part, move_x, x, jnp.zeros((NX, slots, feat), BF))
        both = jnp.stack([mine, swap_core(mine)])
        return both.transpose(0, 2, 1, 3).reshape(2 * slots, D)

    rows_in = all_features(rows_part)
    grad_in = all_features(grad_part)

    full_a = gather_yz(shard_a, z, y).reshape(D, 4 * HD)
    full_b = gather_zy(shard_b, z, y).transpose(1, 0, 2, 3).reshape(D, 4 * HD)

    rows_wide = rows_in.astype(F32)
    inv_scale = lax.rsqrt(jnp.mean(rows_wide * rows_wide, axis=1, keepdims=True) + EPS)
    normed = (rows_wide * inv_scale * gain).astype(BF)
    gate = jax.nn.sigmoid(jnp.sum(rows_wide * w_router, axis=1))
    position, docs = meta[:, 0], meta[:, 1]
    live = meta[:, 2] > 0
    live_flat = live.reshape(-1)
    d_mix = (jnp.where(live_flat, gate, 0.0)[:, None] * grad_in.astype(F32)).astype(BF)

    def project(weight):
        out = jnp.dot(normed, weight[:, : 3 * HD], preferred_element_type=F32).astype(BF)
        return out.reshape(2, slots, 3, HD)

    qkv = jnp.stack([project(full_a), project(full_b)])
    query, key, value = qkv[:, :, :, 0], qkv[:, :, :, 1], qkv[:, :, :, 2]
    scores = (
        jnp.einsum("hsqd,hskd->hsqk", query, key, preferred_element_type=F32) * HD ** (-0.5)
    )
    allowed = (
        (position[:, None, :] <= position[:, :, None])
        & (docs[:, None, :] == docs[:, :, None])
        & live[:, None, :]
    )
    allowed = allowed | jnp.eye(slots, dtype=bool)[None]
    scores = jnp.where(allowed[None], scores, -1e30)
    expo = jnp.exp(scores - jnp.max(scores, axis=3, keepdims=True))
    probs = expo / jnp.sum(expo, axis=3, keepdims=True)
    probs_low = probs.astype(BF)
    attn = jnp.einsum("hsqk,hskd->hsqd", probs_low, value, preferred_element_type=F32).astype(BF)
    attn_flat = attn.reshape(2, 2 * slots, HD)

    grad_a = dot_tn(d_mix, attn_flat[0]).reshape(NZ, NY, 128, HD)
    grad_b = dot_tn(d_mix, attn_flat[1]).reshape(NZ, NY, 128, HD).transpose(1, 0, 2, 3)
    sum_a = reduce_ring4(reduce_ring8(grad_a, z), y, move_y)
    sum_b = reduce_ring8(reduce_ring4(grad_b, y, move_y), z)
    total = jnp.stack([sum_a, sum_b])
    gram = gram_total(
        jnp.einsum("hdi,hdj->hij", total, total, precision=lax.Precision.HIGHEST), z
    )
    eye = jnp.eye(HD, dtype=F32)
    square = jnp.sum(gram * eye, axis=(1, 2))
    inv_norm = (1.0 / (jnp.sqrt(square) + 1e-07))[:, None, None]
    gram = gram * inv_norm * inv_norm
    step = COEF_A * eye + COEF_B * gram + COEF_C * high_dot(gram, gram)
    gram = high_dot(high_dot(step, gram), step)
    step = high_dot(COEF_A * eye + COEF_B * gram + COEF_C * high_dot(gram, gram), step)
    ortho = jnp.einsum(
        "hdj,hij->dhi", total, step * inv_norm, precision=lax.Precision.HIGHEST
    ) * (0.2 * math.sqrt(D))
    ortho = ortho.reshape(2, 64, 256)
    own_cols = lax.dynamic_index_in_dim(ortho, c, 0, keepdims=False)
    other_cols = swap_core(lax.dynamic_index_in_dim(ortho, 1 - c, 0, keepdims=False))
    muon_step = jnp.where(
        c == 0,
        jnp.concatenate([own_cols, other_cols], axis=1),
        jnp.concatenate([other_cols, own_cols], axis=1),
    ).T

    attn_cols = jnp.concatenate([attn_flat[0], attn_flat[1]], axis=1)
    out_cols = jnp.concatenate([full_a[:, 3 * HD :], full_b[:, 3 * HD :]], axis=1)
    out_blocks = out_cols.reshape(NX, feat, 2 * HD)

    def to_owner(piece):
        total = None
        for k in (2, 1, 3, 0):
            part = piece(k)
            got = swap_core(part[slots:].astype(BF))
            part = part[:slots] + got.astype(F32)
            if k:
                part = move_x(part.astype(BF), k).astype(F32)
            total = part if total is None else total + part
        return total

    mixed = to_owner(lambda k: dot_nt(attn_cols, pick(out_blocks, x + k, NX)))

    d_attn = jnp.dot(d_mix, out_cols, preferred_element_type=F32).astype(BF)
    d_heads = d_attn.reshape(2, slots, 2, HD).transpose(2, 0, 1, 3)
    d_probs = jnp.einsum("hsqd,hskd->hsqk", d_heads, value, preferred_element_type=F32)
    row_sum = jnp.sum(d_probs * probs, axis=3, keepdims=True)
    d_scores = (probs * (d_probs - row_sum) * HD ** (-0.5)).astype(BF)
    d_query = jnp.einsum("hsqk,hskd->hsqd", d_scores, key, preferred_element_type=F32).astype(BF)
    d_key = jnp.einsum("hsqk,hsqd->hskd", d_scores, query, preferred_element_type=F32).astype(BF)
    d_value = jnp.einsum(
        "hsqk,hsqd->hskd", probs_low, d_heads, preferred_element_type=F32
    ).astype(BF)

    def wide_dot(left, right):
        return jnp.sum(left.astype(F32) * right.astype(F32), axis=(0, 3))

    gate_sum = wide_dot(attn, d_heads)
    stat_sum = wide_dot(query, d_query) + wide_dot(key, d_key) + wide_dot(value, d_value)
    sums = jnp.stack([gate_sum, stat_sum])
    sums = sums[:, 0] + swap_core(sums[:, 1])
    sums = sums + (move_x(sums, 1) + move_x(sums, -1)) + move_x(sums, 2)

    d_qkv = jnp.concatenate([d_query, d_key, d_value], axis=3).reshape(2, 2 * slots, 3 * HD)
    blocks_a = full_a.reshape(NX, feat, 4 * HD)
    blocks_b = full_b.reshape(NX, feat, 4 * HD)

    def back(k):
        part = dot_nt(d_qkv[0], pick(blocks_a, x + k, NX)[:, : 3 * HD])
        return part + dot_nt(d_qkv[1], pick(blocks_b, x + k, NX)[:, : 3 * HD])

    d_normed = to_owner(back)

    rows_own = rows_part.astype(F32)
    gate_own = gate[:slots]
    inv_own = inv_scale[:slots]
    hit = jnp.any(picks & live_own[:, None], axis=0)[:, None]
    updated = (rows_own + gate_own[:, None] * mixed).astype(BF)

    def spread(values):
        return lax.dot_general(
            onehot, values, (((0,), (0,)), ((), ())), preferred_element_type=F32
        ).astype(BF)

    block_out = jnp.where(hit, spread(updated), tokens)
    gain_local = lax.dynamic_slice_in_dim(gain, x * feat, feat)
    router_local = lax.dynamic_slice_in_dim(w_router, x * feat, feat)
    d_logit = sums[0] * (1.0 - gate_own)
    stat = sums[1][:, None] / D
    d_rows = (
        grad_part.astype(F32)
        + inv_own * (d_normed * gain_local - rows_own * inv_own * stat)
        + d_logit[:, None] * router_local
    )
    token_grad = jnp.where(hit, spread(d_rows.astype(BF)), cotangent)
    return (block_out, token_grad, muon_step)


def solution(mesh):
    placed = (
        P("dp", "mp"),
        P("dp", "mp"),
        P("dp", "mp"),
        P("dp", "mp"),
        P("dp", "mp"),
        P("mp", "dp"),
        P(),
        P(),
        P("dp"),
        P("dp"),
        P("dp"),
    )
    return jax.shard_map(
        per_device,
        mesh=mesh,
        in_specs=placed,
        out_specs=(P("dp", "mp"), P("dp", "mp"), P("mp", "dp")),
        check_vma=False,
    )
```

```python
import math

import jax
import jax.numpy as jnp
from jax import lax
from jax.experimental import pallas as pl
from jax.experimental.pallas import tpu as pltpu
from jax.sharding import PartitionSpec as P

D = 4096
HD = 128
CAP = 128
NZ, NY, NC, NX = 8, 4, 2, 4
FEAT = D // NX
EXTRA = 128
EPS = 1e-06
COEF_A = 3.4445
COEF_B = -4.775
COEF_C = 2.0315
BF = jnp.bfloat16
F32 = jnp.float32
VMEM_LIMIT = 48 * 1024 * 1024


def dp_index(z, y, c):
    return ((z % NZ) * NY + (y % NY)) * NC + c


def dp_perm(dz, dy, dc):
    return [
        (dp_index(z, y, c), dp_index(z + dz, y + dy, (c + dc) % NC))
        for z in range(NZ)
        for y in range(NY)
        for c in range(NC)
    ]


GROUPS_ZY = [[dp_index(z, y, c) for z in range(NZ) for y in range(NY)] for c in range(NC)]
GROUPS_Z = [[dp_index(z, y, c) for z in range(NZ)] for y in range(NY) for c in range(NC)]


def move_y(v, k):
    return lax.ppermute(v, "dp", dp_perm(0, k, 0))


def swap_core(v):
    return lax.ppermute(v, "dp", dp_perm(0, 0, 1))


def move_x(v, k):
    return lax.ppermute(v, "mp", [(i, (i + k) % NX) for i in range(NX)])


def dot_nn(left, right):
    return jnp.dot(left, right, preferred_element_type=F32)


def dot_nt(left, right):
    return lax.dot_general(
        left, right, (((1,), (1,)), ((), ())), preferred_element_type=F32
    )


def dot_tn(left, right):
    return lax.dot_general(
        left, right, (((0,), (0,)), ((), ())), preferred_element_type=F32
    )


def forward_kernel(
    place, normed, d_mix, weight, mask, qkv_out, da_out, attn_out, probs_out, *rest
):
    grads, (qkv_acc, da_acc) = rest[:NY], rest[NY:]
    step = pl.program_id(0)

    @pl.when(step == 0)
    def _():
        qkv_acc[...] = jnp.zeros_like(qkv_acc)
        da_acc[...] = jnp.zeros_like(da_acc)

    qkv_acc[...] += dot_nn(normed[0], weight[:, : 6 * HD])
    x_abs = lax.rem(place[0] + step, NX)
    da_acc[...] += dot_nn(d_mix[x_abs], weight[:, 6 * HD :])

    @pl.when(step == NX - 1)
    def _():
        qkv_out[...] = qkv_acc[...].astype(BF)
        da_out[...] = da_acc[...].astype(BF)
        for s in range(2):
            rows = pl.ds(s * CAP, CAP)
            for h in range(2):
                query = qkv_out[rows, pl.ds(h * HD, HD)]
                key = qkv_out[rows, pl.ds((2 + h) * HD, HD)]
                value = qkv_out[rows, pl.ds((4 + h) * HD, HD)]
                scores = dot_nt(query, key) * HD ** (-0.5)
                scores = jnp.where(mask[rows, :] > 0.0, scores, -1e30)
                expo = jnp.exp(scores - jnp.max(scores, axis=1, keepdims=True))
                probs = expo / jnp.sum(expo, axis=1, keepdims=True)
                probs_out[s, h] = probs
                attn_out[rows, pl.ds(h * HD, HD)] = dot_nn(probs.astype(BF), value).astype(BF)
        attn = attn_out[...]
        for k in range(NY):
            y_abs = lax.rem(place[1] + k, NY)
            for i in range(NX):
                for j in range(2):
                    col = pl.ds(pl.multiple_of(j * 512 + y_abs * 128, 128), 128)
                    grads[k][2 * i + j] = dot_tn(attn, d_mix[i, :, col]).astype(BF)


def forward(place, normed, d_mix, weight, mask):
    whole = lambda *dims: pl.BlockSpec(dims, lambda i, p: (0,) * len(dims))
    return pl.pallas_call(
        forward_kernel,
        grid_spec=pltpu.PrefetchScalarGridSpec(
            num_scalar_prefetch=1,
            grid=(NX,),
            in_specs=[
                pl.BlockSpec((1, 2 * CAP, FEAT), lambda i, p: (lax.rem(p[0] + i, NX), 0, 0)),
                whole(NX, 2 * CAP, FEAT),
                pl.BlockSpec((FEAT, 8 * HD), lambda i, p: (lax.rem(p[0] + i, NX), 0)),
                whole(2 * CAP, CAP),
            ],
            out_specs=[
                whole(2 * CAP, 6 * HD),
                whole(2 * CAP, 2 * HD),
                whole(2 * CAP, 2 * HD),
                whole(2, 2, CAP, CAP),
            ]
            + [whole(NZ, 2 * HD, 128)] * NY,
            scratch_shapes=[
                pltpu.VMEM((2 * CAP, 6 * HD), F32),
                pltpu.VMEM((2 * CAP, 2 * HD), F32),
            ],
        ),
        out_shape=[
            jax.ShapeDtypeStruct((2 * CAP, 6 * HD), BF),
            jax.ShapeDtypeStruct((2 * CAP, 2 * HD), BF),
            jax.ShapeDtypeStruct((2 * CAP, 2 * HD), BF),
            jax.ShapeDtypeStruct((2, 2, CAP, CAP), F32),
        ]
        + [jax.ShapeDtypeStruct((NZ, 2 * HD, 128), BF)] * NY,
        compiler_params=pltpu.CompilerParams(vmem_limit_bytes=VMEM_LIMIT),
        cost_estimate=pl.CostEstimate(
            flops=2 * 256 * 4096 * 1280, bytes_accessed=16 << 20, transcendentals=1 << 16
        ),
        name="forward",
    )(place, normed, d_mix, weight, mask)


def backward_kernel(place, qkv, d_attn, attn, probs_in, weight, own_out, sib_out, d_qkv, sums):
    step = pl.program_id(0)

    @pl.when(step == 0)
    def _():
        lane = lax.broadcasted_iota(jnp.int32, (CAP, EXTRA), 1)
        for s in range(2):
            rows = pl.ds(s * CAP, CAP)
            gate_sum = jnp.zeros((CAP, 1), F32)
            stat_sum = jnp.zeros((CAP, 1), F32)
            for h in range(2):
                query = qkv[rows, pl.ds(h * HD, HD)]
                key = qkv[rows, pl.ds((2 + h) * HD, HD)]
                value = qkv[rows, pl.ds((4 + h) * HD, HD)]
                d_head = d_attn[rows, pl.ds(h * HD, HD)]
                probs = probs_in[s, h]
                d_probs = dot_nt(d_head, value)
                row_sum = jnp.sum(d_probs * probs, axis=1, keepdims=True)
                d_scores = (probs * (d_probs - row_sum) * HD ** (-0.5)).astype(BF)
                d_query = dot_nn(d_scores, key).astype(BF)
                d_key = dot_tn(d_scores, query).astype(BF)
                d_value = dot_tn(probs.astype(BF), d_head).astype(BF)
                d_qkv[rows, pl.ds(h * HD, HD)] = d_query
                d_qkv[rows, pl.ds((2 + h) * HD, HD)] = d_key
                d_qkv[rows, pl.ds((4 + h) * HD, HD)] = d_value
                out = attn[rows, pl.ds(h * HD, HD)]
                gate_sum += jnp.sum(out.astype(F32) * d_head.astype(F32), axis=1, keepdims=True)
                stat_sum += jnp.sum(
                    query.astype(F32) * d_query.astype(F32)
                    + key.astype(F32) * d_key.astype(F32)
                    + value.astype(F32) * d_value.astype(F32),
                    axis=1,
                    keepdims=True,
                )
            sums[s, 0] = jnp.where(lane == 0, gate_sum, 0.0).astype(BF)
            sums[s, 1] = jnp.where(lane == 0, stat_sum, 0.0).astype(BF)

    mixed = dot_nt(attn[...], weight[:, 6 * HD :]).astype(BF)
    d_normed = dot_nt(d_qkv[...], weight[:, : 6 * HD]).astype(BF)
    for s, out in ((0, own_out), (1, sib_out)):
        out[0, 0, :, :FEAT] = mixed[s * CAP : (s + 1) * CAP]
        out[0, 1, :, :FEAT] = d_normed[s * CAP : (s + 1) * CAP]
        out[0, 0, :, FEAT:] = sums[s, 0]
        out[0, 1, :, FEAT:] = sums[s, 1]


def backward(place, qkv, d_attn, attn, probs, weight):
    whole = lambda *dims: pl.BlockSpec(dims, lambda i, p: (0,) * len(dims))
    piece = pl.BlockSpec((1, 2, CAP, FEAT + EXTRA), lambda i, p: (i, 0, 0, 0))
    piece_type = jax.ShapeDtypeStruct((NX, 2, CAP, FEAT + EXTRA), BF)
    return pl.pallas_call(
        backward_kernel,
        grid_spec=pltpu.PrefetchScalarGridSpec(
            num_scalar_prefetch=1,
            grid=(NX,),
            in_specs=[
                whole(2 * CAP, 6 * HD),
                whole(2 * CAP, 2 * HD),
                whole(2 * CAP, 2 * HD),
                whole(2, 2, CAP, CAP),
                pl.BlockSpec((FEAT, 8 * HD), lambda i, p: (lax.rem(p[0] + i, NX), 0)),
            ],
            out_specs=[piece, piece],
            scratch_shapes=[
                pltpu.VMEM((2 * CAP, 6 * HD), BF),
                pltpu.VMEM((2, 2, CAP, EXTRA), BF),
            ],
        ),
        out_shape=[piece_type, piece_type],
        compiler_params=pltpu.CompilerParams(vmem_limit_bytes=VMEM_LIMIT),
        cost_estimate=pl.CostEstimate(
            flops=2 * 256 * 4096 * 1024, bytes_accessed=14 << 20, transcendentals=0
        ),
        name="backward",
    )(place, qkv, d_attn, attn, probs, weight)


def high(left, right, dims):
    return lax.dot_general(
        left,
        right,
        (dims, ((), ())),
        precision=lax.Precision.HIGHEST,
        preferred_element_type=F32,
    )


def gram_kernel(parts, total_out, gram_out):
    total = parts[0].astype(F32)
    for k in range(1, NZ):
        total = total + parts[k].astype(F32)
    total_out[...] = total
    for h in range(2):
        block = total[h * HD : (h + 1) * HD]
        gram_out[h] = high(block, block, ((1,), (1,)))


def gram_of(parts):
    return pl.pallas_call(
        gram_kernel,
        out_shape=[
            jax.ShapeDtypeStruct((2 * HD, 128), F32),
            jax.ShapeDtypeStruct((2, HD, HD), F32),
        ],
        compiler_params=pltpu.CompilerParams(vmem_limit_bytes=VMEM_LIMIT),
        name="gram",
    )(parts)


def muon_kernel(gram_in, total, out):
    row = lax.broadcasted_iota(jnp.int32, (HD, HD), 0)
    col = lax.broadcasted_iota(jnp.int32, (HD, HD), 1)
    eye = jnp.where(row == col, 1.0, 0.0).astype(F32)
    nn = ((1,), (0,))
    for h in range(2):
        gram = gram_in[h]
        diag = jnp.sum(gram * eye, axis=1, keepdims=True)
        inv = 1.0 / (jnp.sqrt(jnp.sum(diag, axis=0, keepdims=True)) + 1e-07)
        gram = gram * inv * inv
        step = COEF_A * eye + COEF_B * gram + COEF_C * high(gram, gram, nn)
        gram = high(high(step, gram, nn), step, nn)
        last = COEF_A * eye + COEF_B * gram + COEF_C * high(gram, gram, nn)
        step = high(last, step, nn) * (inv * (0.2 * math.sqrt(D)))
        block = total[h * HD : (h + 1) * HD]
        out[:, h * HD : (h + 1) * HD] = high(block, step, ((0,), (1,)))


def muon(gram, total):
    return pl.pallas_call(
        muon_kernel,
        out_shape=jax.ShapeDtypeStruct((128, 2 * HD), F32),
        compiler_params=pltpu.CompilerParams(vmem_limit_bytes=VMEM_LIMIT),
        name="muon",
    )(gram, total)


def per_device(
    tokens, cotangent, w_query, w_key, w_value, w_out, gain, w_router, chosen, counts, doc_start
):
    dp = lax.axis_index("dp")
    x = lax.axis_index("mp")
    c = lax.rem(dp, NC)
    y = lax.rem(lax.div(dp, NC), NY)
    place = jnp.stack([x, y]).astype(jnp.int32)

    stacked = jnp.concatenate(
        [w.reshape(64, 2, 2 * HD) for w in (w_query, w_key, w_value, w_out.T)], axis=2
    )
    keep = lax.dynamic_index_in_dim(stacked, c, 1, keepdims=False)
    give = lax.dynamic_index_in_dim(stacked, 1 - c, 1, keepdims=False)
    take = swap_core(give)
    shard = jnp.where(
        c == 0, jnp.concatenate([keep, take]), jnp.concatenate([take, keep])
    )
    weight = lax.all_gather(shard, "dp", axis=0, tiled=True, axis_index_groups=GROUPS_ZY)

    picks = chosen[:, None] == jnp.arange(tokens.shape[0])[None, :]
    onehot = picks.astype(BF)
    live_own = jnp.arange(CAP) < counts[0]
    docs_own = jnp.sum(jnp.where(picks, doc_start[None, :], 0), axis=1)
    rows_part = dot_nn(onehot, tokens).astype(BF)
    grad_part = dot_nn(onehot, cotangent).astype(BF)
    meta_own = jnp.stack([chosen, docs_own, live_own.astype(jnp.int32)])
    meta = jnp.stack([meta_own, swap_core(meta_own)])
    position, docs = meta[:, 0], meta[:, 1]
    live = meta[:, 2] > 0

    part = jnp.stack([rows_part, grad_part])
    around = jnp.stack([part] + [move_x(part, k) for k in (3, 2, 1)])
    both = jnp.stack([around, swap_core(around)], axis=2)
    both = jnp.roll(both, x, axis=0).reshape(NX, 2, 2 * CAP, FEAT)
    rows_wide = both[:, 0].astype(F32)
    grad_wide = both[:, 1].astype(F32)
    gain_parts = gain.reshape(NX, 1, FEAT)
    router_parts = w_router.reshape(NX, 1, FEAT)
    mean_square = jnp.sum(rows_wide * rows_wide, axis=(0, 2)) / D
    inv_scale = lax.rsqrt(mean_square + EPS)[:, None]
    gate = jax.nn.sigmoid(jnp.sum(rows_wide * router_parts, axis=(0, 2)))
    normed = (rows_wide * inv_scale * gain_parts).astype(BF)
    gate_live = jnp.where(live.reshape(-1), gate, 0.0)[:, None]
    d_mix = (gate_live * grad_wide).astype(BF)
    allowed = (
        (position[:, None, :] <= position[:, :, None])
        & (docs[:, None, :] == docs[:, :, None])
        & live[:, None, :]
    )
    allowed = allowed | jnp.eye(CAP, dtype=bool)[None]
    mask = allowed.reshape(2 * CAP, CAP).astype(F32)

    qkv, d_attn, attn, probs, grad_0, grad_1, grad_2, grad_3 = forward(
        place, normed, d_mix, weight, mask
    )
    moved = [move_y(grad_1, 1), move_y(grad_3, 3), move_y(grad_2, 2)]

    own, sibling = backward(place, qkv, d_attn, attn, probs, weight)
    got = swap_core(sibling)
    sent = [
        move_x((own[k].astype(F32) + got[k].astype(F32)).astype(BF), k) for k in (1, 3, 2)
    ]

    column = grad_0.astype(F32)
    for m in moved:
        column = column + m.astype(F32)
    column = lax.all_to_all(
        column.astype(BF), "dp", 0, 0, tiled=True, axis_index_groups=GROUPS_Z
    )
    total, gram = gram_of(column)
    pieces = gram.reshape(NZ * NY, 8, 128)
    pieces = lax.all_to_all(pieces, "dp", 0, 0, tiled=True, axis_index_groups=GROUPS_ZY)
    piece = jnp.broadcast_to(jnp.sum(pieces, axis=0)[None], (NZ * NY, 8, 128))
    gram = lax.all_to_all(piece, "dp", 0, 0, tiled=True, axis_index_groups=GROUPS_ZY)
    ortho = muon(gram.reshape(2, HD, HD), total).reshape(2, 64, 2 * HD)
    own_cols = lax.dynamic_index_in_dim(ortho, c, 0, keepdims=False)
    other_cols = swap_core(lax.dynamic_index_in_dim(ortho, 1 - c, 0, keepdims=False))
    muon_step = jnp.where(
        c == 0,
        jnp.concatenate([own_cols, other_cols], axis=1),
        jnp.concatenate([other_cols, own_cols], axis=1),
    ).T

    result = own[0].astype(F32) + got[0].astype(F32)
    for s in sent:
        result = result + s.astype(F32)
    mixed, d_normed = result[0, :, :FEAT], result[1, :, :FEAT]
    gate_sum, stat_sum = result[0, :, FEAT : FEAT + 1], result[1, :, FEAT : FEAT + 1]
    rows_own = rows_part.astype(F32)
    gate_own = gate[:CAP, None]
    inv_own = inv_scale[:CAP]
    hit = jnp.any(picks & live_own[:, None], axis=0)[:, None]
    updated = (rows_own + gate_own * mixed).astype(BF)

    def spread(values):
        return dot_tn(onehot, values).astype(BF)

    block_out = jnp.where(hit, spread(updated), tokens)
    gain_local = lax.dynamic_slice_in_dim(gain, x * FEAT, FEAT)
    router_local = lax.dynamic_slice_in_dim(w_router, x * FEAT, FEAT)
    d_logit = gate_sum * (1.0 - gate_own)
    d_rows = (
        grad_part.astype(F32)
        + inv_own * (d_normed * gain_local - rows_own * inv_own * (stat_sum / D))
        + d_logit * router_local
    )
    token_grad = jnp.where(hit, spread(d_rows.astype(BF)), cotangent)
    return (block_out, token_grad, muon_step)


def solution(mesh):
    placed = (
        P("dp", "mp"),
        P("dp", "mp"),
        P("dp", "mp"),
        P("dp", "mp"),
        P("dp", "mp"),
        P("mp", "dp"),
        P(),
        P(),
        P("dp"),
        P("dp"),
        P("dp"),
    )
    return jax.shard_map(
        per_device,
        mesh=mesh,
        in_specs=placed,
        out_specs=(P("dp", "mp"), P("dp", "mp"), P("mp", "dp")),
        check_vma=False,
    )
```

```python
import math

import jax
import jax.numpy as jnp
from jax import lax
from jax.experimental import pallas as pl
from jax.experimental.pallas import tpu as pltpu
from jax.sharding import PartitionSpec as P

D = 4096
HD = 128
CAP = 128
NZ, NY, NC, NX = 8, 4, 2, 4
FEAT = D // NX
EXTRA = 128
EPS = 1e-06
COEF_A = 3.4445
COEF_B = -4.775
COEF_C = 2.0315
BF = jnp.bfloat16
F32 = jnp.float32
VMEM_LIMIT = 60 * 1024 * 1024
SMALL_LIMIT = 16 * 1024 * 1024


def dp_index(z, y, c):
    return ((z % NZ) * NY + (y % NY)) * NC + c


def dp_perm(dz, dy, dc):
    return [
        (dp_index(z, y, c), dp_index(z + dz, y + dy, (c + dc) % NC))
        for z in range(NZ)
        for y in range(NY)
        for c in range(NC)
    ]


GROUPS_ZY = [[dp_index(z, y, c) for z in range(NZ) for y in range(NY)] for c in range(NC)]
GROUPS_Z = [[dp_index(z, y, c) for z in range(NZ)] for y in range(NY) for c in range(NC)]


def after(value, *others):
    return lax.optimization_barrier((value,) + others)[0]


def move_y(v, k):
    return lax.ppermute(v, "dp", dp_perm(0, k, 0))


def swap_core(v):
    return lax.ppermute(v, "dp", dp_perm(0, 0, 1))


def move_x(v, k):
    return lax.ppermute(v, "mp", [(i, (i + k) % NX) for i in range(NX)])


def dot_nn(left, right):
    return jnp.dot(left, right, preferred_element_type=F32)


def dot_nt(left, right):
    return lax.dot_general(
        left, right, (((1,), (1,)), ((), ())), preferred_element_type=F32
    )


def dot_tn(left, right):
    return lax.dot_general(
        left, right, (((0,), (0,)), ((), ())), preferred_element_type=F32
    )


def chunk_of(step, place):
    return lax.rem(place[0] + step, NX)


def forward_kernel(
    place, normed, d_mix, weight, mask, qkv_out, da_out, attn_out, probs_out, *rest
):
    grads, (qkv_acc, da_acc, kept) = rest[:NY], rest[NY:]
    step = pl.program_id(0)

    @pl.when(step == 0)
    def _():
        qkv_acc[...] = jnp.zeros_like(qkv_acc)
        da_acc[...] = jnp.zeros_like(da_acc)

    qkv_acc[...] += dot_nn(normed[0], weight[:, : 6 * HD])
    da_acc[...] += dot_nn(d_mix[0], weight[:, 6 * HD :])
    kept[chunk_of(step, place)] = d_mix[0]

    @pl.when(step == NX - 1)
    def _():
        qkv_out[...] = qkv_acc[...].astype(BF)
        da_out[...] = da_acc[...].astype(BF)
        for s in range(2):
            rows = pl.ds(s * CAP, CAP)
            for h in range(2):
                query = qkv_out[rows, pl.ds(h * HD, HD)]
                key = qkv_out[rows, pl.ds((2 + h) * HD, HD)]
                value = qkv_out[rows, pl.ds((4 + h) * HD, HD)]
                scores = dot_nt(query, key) * HD ** (-0.5)
                scores = jnp.where(mask[rows, :] > 0.0, scores, -1e30)
                expo = jnp.exp(scores - jnp.max(scores, axis=1, keepdims=True))
                probs = expo / jnp.sum(expo, axis=1, keepdims=True)
                probs_out[s, h] = probs
                attn_out[rows, pl.ds(h * HD, HD)] = dot_nn(probs.astype(BF), value).astype(BF)
        row = lax.broadcasted_iota(jnp.int32, (2 * CAP, 2 * CAP), 0)
        col = lax.broadcasted_iota(jnp.int32, (2 * CAP, 2 * CAP), 1)
        eye = jnp.where(row == col, 1.0, 0.0).astype(BF)
        attn_t = dot_tn(attn_out[...], eye).astype(BF)
        for k in range(NY):
            y_abs = lax.rem(place[1] + k, NY)
            for i in range(NX):
                low = kept[i, :, pl.ds(pl.multiple_of(y_abs * 128, 128), 128)]
                high = kept[i, :, pl.ds(pl.multiple_of(512 + y_abs * 128, 128), 128)]
                res = dot_nn(attn_t, jnp.concatenate([low, high], axis=1)).astype(BF)
                grads[k][2 * i] = res[:, :128]
                grads[k][2 * i + 1] = res[:, 128:]


def forward(place, normed, d_mix, weight, mask):
    whole = lambda *dims: pl.BlockSpec(dims, lambda i, p: (0,) * len(dims))
    rows = pl.BlockSpec(
        (1, 2 * CAP, FEAT), lambda i, p: (chunk_of(i, p), 0, 0)
    )
    return pl.pallas_call(
        forward_kernel,
        grid_spec=pltpu.PrefetchScalarGridSpec(
            num_scalar_prefetch=1,
            grid=(NX,),
            in_specs=[
                rows,
                rows,
                pl.BlockSpec((FEAT, 8 * HD), lambda i, p: (chunk_of(i, p), 0)),
                whole(2 * CAP, CAP),
            ],
            out_specs=[
                whole(2 * CAP, 6 * HD),
                whole(2 * CAP, 2 * HD),
                whole(2 * CAP, 2 * HD),
                whole(2, 2, CAP, CAP),
            ]
            + [whole(NZ, 2 * HD, 128)] * NY,
            scratch_shapes=[
                pltpu.VMEM((2 * CAP, 6 * HD), F32),
                pltpu.VMEM((2 * CAP, 2 * HD), F32),
                pltpu.VMEM((NX, 2 * CAP, FEAT), BF),
            ],
        ),
        out_shape=[
            jax.ShapeDtypeStruct((2 * CAP, 6 * HD), BF),
            jax.ShapeDtypeStruct((2 * CAP, 2 * HD), BF),
            jax.ShapeDtypeStruct((2 * CAP, 2 * HD), BF),
            jax.ShapeDtypeStruct((2, 2, CAP, CAP), F32),
        ]
        + [pltpu.HBM((NZ, 2 * HD, 128), BF)] * NY,
        compiler_params=pltpu.CompilerParams(vmem_limit_bytes=VMEM_LIMIT),
        cost_estimate=pl.CostEstimate(
            flops=2 * 256 * 4096 * 1280, bytes_accessed=16 << 20, transcendentals=1 << 16
        ),
        name="forward",
    )(place, normed, d_mix, weight, mask)


def backward_kernel(place, qkv, d_attn, attn, probs_in, weight, own_out, sib_out, d_qkv, sums):
    step = pl.program_id(0)

    @pl.when(step == 0)
    def _():
        lane = lax.broadcasted_iota(jnp.int32, (CAP, EXTRA), 1)
        for s in range(2):
            rows = pl.ds(s * CAP, CAP)
            gate_sum = jnp.zeros((CAP, 1), F32)
            stat_sum = jnp.zeros((CAP, 1), F32)
            for h in range(2):
                query = qkv[rows, pl.ds(h * HD, HD)]
                key = qkv[rows, pl.ds((2 + h) * HD, HD)]
                value = qkv[rows, pl.ds((4 + h) * HD, HD)]
                d_head = d_attn[rows, pl.ds(h * HD, HD)]
                probs = probs_in[s, h]
                d_probs = dot_nt(d_head, value)
                row_sum = jnp.sum(d_probs * probs, axis=1, keepdims=True)
                d_scores = (probs * (d_probs - row_sum) * HD ** (-0.5)).astype(BF)
                d_query = dot_nn(d_scores, key).astype(BF)
                d_key = dot_tn(d_scores, query).astype(BF)
                d_value = dot_tn(probs.astype(BF), d_head).astype(BF)
                d_qkv[rows, pl.ds(h * HD, HD)] = d_query
                d_qkv[rows, pl.ds((2 + h) * HD, HD)] = d_key
                d_qkv[rows, pl.ds((4 + h) * HD, HD)] = d_value
                out = attn[rows, pl.ds(h * HD, HD)]
                gate_sum += jnp.sum(out.astype(F32) * d_head.astype(F32), axis=1, keepdims=True)
                stat_sum += jnp.sum(
                    query.astype(F32) * d_query.astype(F32)
                    + key.astype(F32) * d_key.astype(F32)
                    + value.astype(F32) * d_value.astype(F32),
                    axis=1,
                    keepdims=True,
                )
            sums[s, 0] = jnp.where(lane == 0, gate_sum, 0.0).astype(BF)
            sums[s, 1] = jnp.where(lane == 0, stat_sum, 0.0).astype(BF)

    mixed = dot_nt(attn[...], weight[:, 6 * HD :]).astype(BF)
    d_normed = dot_nt(d_qkv[...], weight[:, : 6 * HD]).astype(BF)
    for s, out in ((0, own_out), (1, sib_out)):
        out[0, 0, :, :FEAT] = mixed[s * CAP : (s + 1) * CAP]
        out[0, 1, :, :FEAT] = d_normed[s * CAP : (s + 1) * CAP]
        out[0, 0, :, FEAT:] = sums[s, 0]
        out[0, 1, :, FEAT:] = sums[s, 1]


def backward(place, qkv, d_attn, attn, probs, weight):
    whole = lambda *dims: pl.BlockSpec(dims, lambda i, p: (0,) * len(dims))
    piece = pl.BlockSpec((1, 2, CAP, FEAT + EXTRA), lambda i, p: (i, 0, 0, 0))
    piece_type = pltpu.HBM((NX, 2, CAP, FEAT + EXTRA), BF)
    return pl.pallas_call(
        backward_kernel,
        grid_spec=pltpu.PrefetchScalarGridSpec(
            num_scalar_prefetch=1,
            grid=(NX,),
            in_specs=[
                whole(2 * CAP, 6 * HD),
                whole(2 * CAP, 2 * HD),
                whole(2 * CAP, 2 * HD),
                whole(2, 2, CAP, CAP),
                pl.BlockSpec((FEAT, 8 * HD), lambda i, p: (lax.rem(p[0] + i, NX), 0)),
            ],
            out_specs=[piece, piece],
            scratch_shapes=[
                pltpu.VMEM((2 * CAP, 6 * HD), BF),
                pltpu.VMEM((2, 2, CAP, EXTRA), BF),
            ],
        ),
        out_shape=[piece_type, piece_type],
        compiler_params=pltpu.CompilerParams(vmem_limit_bytes=VMEM_LIMIT),
        cost_estimate=pl.CostEstimate(
            flops=2 * 256 * 4096 * 1024, bytes_accessed=14 << 20, transcendentals=0
        ),
        name="backward",
    )(place, qkv, d_attn, attn, probs, weight)


def stack_kernel(*refs):
    out = refs[-1]
    for j, block in enumerate(refs[:-1]):
        out[j] = block[...]


def stack(*blocks):
    whole = pl.BlockSpec(memory_space=pltpu.VMEM)
    return pl.pallas_call(
        stack_kernel,
        in_specs=[whole] * len(blocks),
        out_specs=whole,
        out_shape=jax.ShapeDtypeStruct((len(blocks),) + blocks[0].shape, BF),
        name="stack",
    )(*blocks)


def prep_kernel(place, mine, other, gain, router, live, normed, d_mix, stats):
    lane = lax.broadcasted_iota(jnp.int32, (CAP, 128), 1)
    for s, source in ((0, mine), (1, other)):
        rows = pl.ds(s * CAP, CAP)
        square = jnp.zeros((CAP, 1), F32)
        logit = jnp.zeros((CAP, 1), F32)
        for k in range(NX):
            x_abs = lax.rem(place[0] + k, NX)
            wide = source[k, 0].astype(F32)
            square += jnp.sum(wide * wide, axis=1, keepdims=True)
            logit += jnp.sum(wide * router[x_abs], axis=1, keepdims=True)
        inv = lax.rsqrt(square / D + EPS)
        gate = jax.nn.sigmoid(logit)
        stats[rows, :] = jnp.where(lane == 0, gate, inv)
        gate_live = jnp.where(live[rows, :] > 0.0, gate, 0.0)
        for k in range(NX):
            x_abs = lax.rem(place[0] + k, NX)
            wide = source[k, 0].astype(F32)
            normed[x_abs, rows, :] = (wide * inv * gain[x_abs]).astype(BF)
            d_mix[x_abs, rows, :] = (gate_live * source[k, 1].astype(F32)).astype(BF)


def prep(place, mine, other, gain, router, live):
    whole = pl.BlockSpec(memory_space=pltpu.VMEM)
    return pl.pallas_call(
        prep_kernel,
        in_specs=[pl.BlockSpec(memory_space=pltpu.SMEM)] + [whole] * 5,
        out_specs=[whole] * 3,
        out_shape=[
            jax.ShapeDtypeStruct((NX, 2 * CAP, FEAT), BF),
            jax.ShapeDtypeStruct((NX, 2 * CAP, FEAT), BF),
            jax.ShapeDtypeStruct((2 * CAP, 128), F32),
        ],
        compiler_params=pltpu.CompilerParams(vmem_limit_bytes=24 * 1024 * 1024),
        name="prep",
    )(place, mine, other, gain, router, live)


def pack_kernel(place, w_query, w_key, w_value, w_out, keep, give):
    for i, w in enumerate((w_query, w_key, w_value, w_out)):
        col = pl.ds(i * 2 * HD, 2 * HD)
        low, high = w[:, : 2 * HD], w[:, 2 * HD :]

        @pl.when(place[2] == 0)
        def _():
            keep[:, col] = low
            give[:, col] = high

        @pl.when(place[2] != 0)
        def _():
            keep[:, col] = high
            give[:, col] = low


def pack(place, *weights):
    whole = pl.BlockSpec(memory_space=pltpu.VMEM)
    return pl.pallas_call(
        pack_kernel,
        in_specs=[pl.BlockSpec(memory_space=pltpu.SMEM)] + [whole] * 4,
        out_specs=[whole] * 2,
        out_shape=[jax.ShapeDtypeStruct((64, 8 * HD), BF)] * 2,
        name="pack",
    )(place, *weights)


def finish_kernel(
    place, own, got, sent_1, sent_2, sent_3, part, stats, gain, router, slots, tokens,
    cotangent, block_out, token_grad, updated, d_rows,
):
    step = pl.program_id(0)

    @pl.when(step == 0)
    def _():
        def summed(kind, cols):
            total = own[0, kind, :, cols].astype(F32) + got[0, kind, :, cols].astype(F32)
            for block in (sent_1, sent_2, sent_3):
                total += block[kind, :, cols].astype(F32)
            return total

        extra = pl.ds(FEAT, EXTRA)
        gate, inv = stats[:, :1], stats[:, 1:2]
        d_logit = summed(0, extra)[:, :1] * (1.0 - gate)
        stat = summed(1, extra)[:, :1] / D
        for j in range(0, FEAT, 256):
            cols = pl.ds(j, 256)
            rows = part[0, :, cols].astype(F32)
            updated[:, cols] = (rows + gate * summed(0, cols)).astype(BF)
            value = summed(1, cols) * gain[0, :, cols] - rows * inv * stat
            value = part[1, :, cols].astype(F32) + inv * value + d_logit * router[0, :, cols]
            d_rows[:, cols] = value.astype(BF)

    height = tokens.shape[0]
    row = lax.broadcasted_iota(jnp.int32, (height, CAP), 0) + step * height
    hits = jnp.where(row == slots[...], 1.0, 0.0)
    hit = jnp.sum(hits, axis=1, keepdims=True) > 0.0
    hits = hits.astype(BF)
    block_out[...] = jnp.where(hit, dot_nn(hits, updated[...]).astype(BF), tokens[...])
    token_grad[...] = jnp.where(hit, dot_nn(hits, d_rows[...]).astype(BF), cotangent[...])


def finish(place, own, got, sent, part, stats, gain, router, slots, tokens, cotangent):
    whole = lambda *dims: pl.BlockSpec(dims, lambda i, p: (0,) * len(dims))
    local = pl.BlockSpec((1, 1, FEAT), lambda i, p: (p[0], 0, 0))
    rows = tokens.shape[0]
    tile = pl.BlockSpec((rows // 4, FEAT), lambda i, p: (i, 0))
    piece = whole(1, 2, CAP, FEAT + EXTRA)
    return pl.pallas_call(
        finish_kernel,
        grid_spec=pltpu.PrefetchScalarGridSpec(
            num_scalar_prefetch=1,
            grid=(4,),
            in_specs=[piece, piece]
            + [whole(2, CAP, FEAT + EXTRA)] * 3
            + [whole(2, CAP, FEAT), whole(CAP, 128), local, local, whole(1, CAP), tile, tile],
            out_specs=[tile, tile],
            scratch_shapes=[pltpu.VMEM((CAP, FEAT), BF)] * 2,
        ),
        out_shape=[
            pltpu.HBM((rows, FEAT), BF),
            pltpu.HBM((rows, FEAT), BF),
        ],
        compiler_params=pltpu.CompilerParams(vmem_limit_bytes=VMEM_LIMIT),
        cost_estimate=pl.CostEstimate(
            flops=4 * rows * FEAT * CAP, bytes_accessed=11 << 20, transcendentals=0
        ),
        name="finish",
    )(place, own, got, *sent, part, stats, gain, router, slots, tokens, cotangent)


def high(left, right, dims):
    return lax.dot_general(
        left,
        right,
        (dims, ((), ())),
        precision=lax.Precision.HIGHEST,
        preferred_element_type=F32,
    )


def add_kernel(*refs):
    out = refs[-1]
    for j in range(out.shape[0]):
        total = refs[0][j].astype(F32)
        for block in refs[1:-1]:
            total = total + block[j].astype(F32)
        out[j] = total.astype(BF)


def add_up(*blocks):
    whole = pl.BlockSpec(memory_space=pltpu.VMEM)
    return pl.pallas_call(
        add_kernel,
        in_specs=[whole] * len(blocks),
        out_specs=whole,
        out_shape=jax.ShapeDtypeStruct(blocks[0].shape, BF),
        compiler_params=pltpu.CompilerParams(vmem_limit_bytes=SMALL_LIMIT),
        name="add",
    )(*blocks)


def gram_kernel(parts, total_out, gram_out):
    total = parts[0].astype(F32)
    for k in range(1, NZ):
        total = total + parts[k].astype(F32)
    total_out[...] = total
    for h in range(2):
        block = total[h * HD : (h + 1) * HD]
        gram_out[h] = high(block, block, ((1,), (1,)))


def gram_of(parts):
    return pl.pallas_call(
        gram_kernel,
        out_shape=[
            jax.ShapeDtypeStruct((2 * HD, 128), F32),
            jax.ShapeDtypeStruct((2, HD, HD), F32),
        ],
        compiler_params=pltpu.CompilerParams(vmem_limit_bytes=SMALL_LIMIT),
        name="gram",
    )(parts)


def total_kernel(pieces, out):
    total = pieces[0]
    for k in range(1, NZ * NY):
        total = total + pieces[k]
    for k in range(NZ * NY):
        out[k] = total


def total_of(pieces):
    return pl.pallas_call(
        total_kernel,
        out_shape=jax.ShapeDtypeStruct(pieces.shape, F32),
        name="total",
    )(pieces)


def muon_kernel(gram_in, total, out):
    row = lax.broadcasted_iota(jnp.int32, (HD, HD), 0)
    col = lax.broadcasted_iota(jnp.int32, (HD, HD), 1)
    eye = jnp.where(row == col, 1.0, 0.0).astype(F32)
    nn = ((1,), (0,))
    for h in range(2):
        gram = gram_in[h]
        diag = jnp.sum(gram * eye, axis=1, keepdims=True)
        inv = 1.0 / (jnp.sqrt(jnp.sum(diag, axis=0, keepdims=True)) + 1e-07)
        gram = gram * inv * inv
        step = COEF_A * eye + COEF_B * gram + COEF_C * high(gram, gram, nn)
        gram = high(high(step, gram, nn), step, nn)
        last = COEF_A * eye + COEF_B * gram + COEF_C * high(gram, gram, nn)
        step = high(last, step, nn) * (inv * (0.2 * math.sqrt(D)))
        block = total[h * HD : (h + 1) * HD]
        out[:, h * HD : (h + 1) * HD] = high(block, step, ((0,), (1,)))


def muon(gram, total):
    return pl.pallas_call(
        muon_kernel,
        out_shape=jax.ShapeDtypeStruct((128, 2 * HD), F32),
        compiler_params=pltpu.CompilerParams(vmem_limit_bytes=SMALL_LIMIT),
        name="muon",
    )(gram, total)


def per_device(
    tokens, cotangent, w_query, w_key, w_value, w_out, gain, w_router, chosen, counts, doc_start
):
    dp = lax.axis_index("dp")
    x = lax.axis_index("mp")
    c = lax.rem(dp, NC)
    y = lax.rem(lax.div(dp, NC), NY)
    place = jnp.stack([x, y, c]).astype(jnp.int32)

    keep, give = pack(place, w_query, w_key, w_value, w_out.T)
    take = swap_core(give)
    shard = jnp.where(
        c == 0, jnp.concatenate([keep, take]), jnp.concatenate([take, keep])
    )
    weight = lax.all_gather(shard, "dp", axis=0, tiled=True, axis_index_groups=GROUPS_ZY)

    picks = chosen[:, None] == jnp.arange(tokens.shape[0])[None, :]
    onehot = picks.astype(BF)
    live_own = jnp.arange(CAP) < counts[0]
    docs_own = jnp.sum(jnp.where(picks, doc_start[None, :], 0), axis=1)
    rows_part = dot_nn(onehot, tokens).astype(BF)
    grad_part = dot_nn(onehot, cotangent).astype(BF)
    meta_own = jnp.stack([chosen, docs_own, live_own.astype(jnp.int32)])
    meta = jnp.stack([meta_own, swap_core(meta_own)])
    position, docs = meta[:, 0], meta[:, 1]
    live = meta[:, 2] > 0

    part = jnp.stack([rows_part, grad_part])
    around = stack(part, *[move_x(part, k) for k in (3, 2, 1)])
    normed, d_mix, stats = prep(
        place,
        around,
        swap_core(around),
        gain.reshape(NX, 1, FEAT),
        w_router.reshape(NX, 1, FEAT),
        live.reshape(2 * CAP, 1).astype(F32),
    )
    allowed = (
        (position[:, None, :] <= position[:, :, None])
        & (docs[:, None, :] == docs[:, :, None])
        & live[:, None, :]
    )
    allowed = allowed | jnp.eye(CAP, dtype=bool)[None]
    mask = allowed.reshape(2 * CAP, CAP).astype(F32)

    qkv, d_attn, attn, probs, grad_0, grad_1, grad_2, grad_3 = forward(
        place, normed, d_mix, weight, mask
    )
    moved = [move_y(grad_1, 1), move_y(grad_3, 3), move_y(grad_2, 2)]

    own, sibling = backward(place, qkv, d_attn, attn, probs, weight)
    sibling = after(sibling, *moved)
    got = swap_core(sibling)
    sums = [(own[k].astype(F32) + got[k].astype(F32)).astype(BF) for k in (1, 3, 2)]

    column = add_up(grad_0, *moved)
    sent = [move_x(v, k) for v, k in zip(sums, (1, 3, 2))]
    column = lax.all_to_all(column, "dp", 0, 0, tiled=True, axis_index_groups=GROUPS_Z)
    total, gram = gram_of(column)
    pieces = gram.reshape(NZ * NY, 8, 128)
    pieces = lax.all_to_all(pieces, "dp", 0, 0, tiled=True, axis_index_groups=GROUPS_ZY)
    pieces = total_of(pieces)
    pieces, *sent = lax.optimization_barrier((pieces, *sent))
    gram = lax.all_to_all(pieces, "dp", 0, 0, tiled=True, axis_index_groups=GROUPS_ZY)
    block_out, token_grad = finish(
        place,
        own,
        got,
        sent,
        part,
        stats,
        gain.reshape(NX, 1, FEAT),
        w_router.reshape(NX, 1, FEAT),
        jnp.where(live_own, chosen, -1)[None],
        tokens,
        cotangent,
    )
    gram, block_out, token_grad = lax.optimization_barrier((gram, block_out, token_grad))
    ortho = muon(gram.reshape(2, HD, HD), total).reshape(2, 64, 2 * HD)
    own_cols = lax.dynamic_index_in_dim(ortho, c, 0, keepdims=False)
    other_cols = swap_core(lax.dynamic_index_in_dim(ortho, 1 - c, 0, keepdims=False))
    muon_step = jnp.where(
        c == 0,
        jnp.concatenate([own_cols, other_cols], axis=1),
        jnp.concatenate([other_cols, own_cols], axis=1),
    ).T

    return (block_out, token_grad, muon_step)


def solution(mesh):
    placed = (
        P("dp", "mp"),
        P("dp", "mp"),
        P("dp", "mp"),
        P("dp", "mp"),
        P("dp", "mp"),
        P("mp", "dp"),
        P(),
        P(),
        P("dp"),
        P("dp"),
        P("dp"),
    )
    return jax.shard_map(
        per_device,
        mesh=mesh,
        in_specs=placed,
        out_specs=(P("dp", "mp"), P("dp", "mp"), P("mp", "dp")),
        check_vma=False,
    )
```

```python
import math

import jax
import jax.numpy as jnp
from jax import lax
from jax.experimental import pallas as pl
from jax.experimental.pallas import tpu as pltpu
from jax.sharding import PartitionSpec as P

D = 4096
HD = 128
CAP = 128
NZ, NY, NC, NX = 8, 4, 2, 4
FEAT = D // NX
EXTRA = 128
EPS = 1e-06
COEF_A = 3.4445
COEF_B = -4.775
COEF_C = 2.0315
BF = jnp.bfloat16
F32 = jnp.float32
VMEM_LIMIT = 60 * 1024 * 1024
SMALL_LIMIT = 16 * 1024 * 1024


def dp_index(z, y, c):
    return ((z % NZ) * NY + (y % NY)) * NC + c


def dp_perm(dz, dy, dc):
    return [
        (dp_index(z, y, c), dp_index(z + dz, y + dy, (c + dc) % NC))
        for z in range(NZ)
        for y in range(NY)
        for c in range(NC)
    ]


GROUPS_ZY = [[dp_index(z, y, c) for z in range(NZ) for y in range(NY)] for c in range(NC)]
GROUPS_Z = [[dp_index(z, y, c) for z in range(NZ)] for y in range(NY) for c in range(NC)]


def after(value, *others):
    return lax.optimization_barrier((value,) + others)[0]


def move_y(v, k):
    return lax.ppermute(v, "dp", dp_perm(0, k, 0))


def swap_core(v):
    return lax.ppermute(v, "dp", dp_perm(0, 0, 1))


def move_x(v, k):
    return lax.ppermute(v, "mp", [(i, (i + k) % NX) for i in range(NX)])


def dot_nn(left, right):
    return jnp.dot(left, right, preferred_element_type=F32)


def dot_nt(left, right):
    return lax.dot_general(
        left, right, (((1,), (1,)), ((), ())), preferred_element_type=F32
    )


def dot_tn(left, right):
    return lax.dot_general(
        left, right, (((0,), (0,)), ((), ())), preferred_element_type=F32
    )


def chunk_of(step, place):
    return lax.rem(place[0] + step, NX)


def forward_kernel(
    place, normed, d_mix, weight, mask, qkv_out, attn_out, probs_out, *rest
):
    grads, (rows_v, mix_v, weight_v, qkv_acc, held, in_sems, out_sems) = rest[:NY], rest[NY:]
    x, y = place[0], place[1]
    cols = pl.ds(pl.multiple_of(place[2] * 6 * HD, 6 * HD), 6 * HD)

    def copies(k):
        chunk = chunk_of(k, place)
        rows = pl.ds(pl.multiple_of(chunk * FEAT, FEAT), FEAT)
        return (
            pltpu.make_async_copy(weight.at[rows, cols], weight_v.at[k], in_sems.at[0, k]),
            pltpu.make_async_copy(normed.at[chunk], rows_v.at[k], in_sems.at[1, k]),
            pltpu.make_async_copy(d_mix.at[chunk], mix_v.at[k], in_sems.at[2, k]),
        )

    fetch = [copies(k) for k in range(NX)]
    for k in range(NX):
        fetch[k][0].start()
        fetch[k][1].start()
    for k in range(NX):
        fetch[k][2].start()
    for k in range(NX):
        fetch[k][0].wait()
        fetch[k][1].wait()
        part = dot_nn(rows_v[k], weight_v[k])
        if k == 0:
            qkv_acc[...] = part
        else:
            qkv_acc[...] += part

    qkv_out[...] = qkv_acc[...].astype(BF)
    for s in range(2):
        rows = pl.ds(s * CAP, CAP)
        for h in range(2):
            query = qkv_out[rows, pl.ds(h * HD, HD)]
            key = qkv_out[rows, pl.ds((2 + h) * HD, HD)]
            value = qkv_out[rows, pl.ds((4 + h) * HD, HD)]
            scores = dot_nt(query, key) * HD ** (-0.5)
            scores = jnp.where(mask[rows, :] > 0.0, scores, -1e30)
            expo = jnp.exp(scores - jnp.max(scores, axis=1, keepdims=True))
            probs = expo / jnp.sum(expo, axis=1, keepdims=True)
            probs_out[s, h] = probs
            attn_out[rows, pl.ds(h * HD, HD)] = dot_nn(probs.astype(BF), value).astype(BF)
    row = lax.broadcasted_iota(jnp.int32, (2 * CAP, 2 * CAP), 0)
    col = lax.broadcasted_iota(jnp.int32, (2 * CAP, 2 * CAP), 1)
    eye = jnp.where(row == col, 1.0, 0.0).astype(BF)
    attn_t = dot_tn(attn_out[...], eye).astype(BF)
    for k in range(NX):
        fetch[k][2].wait()
    sends = [pltpu.make_async_copy(held.at[k], grads[k], out_sems.at[k]) for k in range(NY)]
    for k in (2, 1, 3, 0):
        y_abs = lax.rem(y + k, NY)
        for i in range(NX):
            low = mix_v[i, :, pl.ds(pl.multiple_of(y_abs * 128, 128), 128)]
            high = mix_v[i, :, pl.ds(pl.multiple_of(512 + y_abs * 128, 128), 128)]
            res = dot_nn(attn_t, jnp.concatenate([low, high], axis=1)).astype(BF)
            x_abs = lax.rem(x + i, NX)
            held[k, 2 * x_abs] = res[:, :128]
            held[k, 2 * x_abs + 1] = res[:, 128:]
        sends[k].start()
    for k in range(NY):
        sends[k].wait()


def forward(place, normed, d_mix, weight, mask):
    whole = pl.BlockSpec(memory_space=pltpu.VMEM)
    outside = pl.BlockSpec(memory_space=pl.ANY)
    return pl.pallas_call(
        forward_kernel,
        in_specs=[pl.BlockSpec(memory_space=pltpu.SMEM)] + [outside] * 3 + [whole],
        out_specs=[whole] * 3 + [outside] * NY,
        scratch_shapes=[
            pltpu.VMEM((NX, 2 * CAP, FEAT), BF),
            pltpu.VMEM((NX, 2 * CAP, FEAT), BF),
            pltpu.VMEM((NX, FEAT, 6 * HD), BF),
            pltpu.VMEM((2 * CAP, 6 * HD), F32),
            pltpu.VMEM((NY, NZ, 2 * HD, 128), BF),
            pltpu.SemaphoreType.DMA((3, NX)),
            pltpu.SemaphoreType.DMA((NY,)),
        ],
        out_shape=[
            jax.ShapeDtypeStruct((2 * CAP, 6 * HD), BF),
            jax.ShapeDtypeStruct((2 * CAP, 2 * HD), BF),
            jax.ShapeDtypeStruct((2, 2, CAP, CAP), F32),
        ]
        + [pltpu.HBM((NZ, 2 * HD, 128), BF)] * NY,
        compiler_params=pltpu.CompilerParams(vmem_limit_bytes=VMEM_LIMIT),
        cost_estimate=pl.CostEstimate(
            flops=2 * 256 * 4096 * 1024, bytes_accessed=13 << 20, transcendentals=1 << 16
        ),
        name="forward",
    )(place, normed, d_mix, weight, mask)


def backward_kernel(
    place, qkv, d_mix, out_all, attn, probs_in, weight, out_weight,
    own_out, sib_out, d_qkv, sums, d_attn,
):
    step = pl.program_id(0)

    @pl.when(step == 0)
    def _():
        total = dot_nn(d_mix[0], out_all[:FEAT])
        for i in range(1, NX):
            total += dot_nn(d_mix[i], out_all[i * FEAT : (i + 1) * FEAT])
        d_attn[...] = total.astype(BF)
        lane = lax.broadcasted_iota(jnp.int32, (CAP, EXTRA), 1)
        for s in range(2):
            rows = pl.ds(s * CAP, CAP)
            gate_sum = jnp.zeros((CAP, 1), F32)
            stat_sum = jnp.zeros((CAP, 1), F32)
            for h in range(2):
                query = qkv[rows, pl.ds(h * HD, HD)]
                key = qkv[rows, pl.ds((2 + h) * HD, HD)]
                value = qkv[rows, pl.ds((4 + h) * HD, HD)]
                d_head = d_attn[rows, pl.ds(h * HD, HD)]
                probs = probs_in[s, h]
                d_probs = dot_nt(d_head, value)
                row_sum = jnp.sum(d_probs * probs, axis=1, keepdims=True)
                d_scores = (probs * (d_probs - row_sum) * HD ** (-0.5)).astype(BF)
                d_query = dot_nn(d_scores, key).astype(BF)
                d_key = dot_tn(d_scores, query).astype(BF)
                d_value = dot_tn(probs.astype(BF), d_head).astype(BF)
                d_qkv[rows, pl.ds(h * HD, HD)] = d_query
                d_qkv[rows, pl.ds((2 + h) * HD, HD)] = d_key
                d_qkv[rows, pl.ds((4 + h) * HD, HD)] = d_value
                out = attn[rows, pl.ds(h * HD, HD)]
                gate_sum += jnp.sum(out.astype(F32) * d_head.astype(F32), axis=1, keepdims=True)
                stat_sum += jnp.sum(
                    query.astype(F32) * d_query.astype(F32)
                    + key.astype(F32) * d_key.astype(F32)
                    + value.astype(F32) * d_value.astype(F32),
                    axis=1,
                    keepdims=True,
                )
            sums[s, 0] = jnp.where(lane == 0, gate_sum, 0.0).astype(BF)
            sums[s, 1] = jnp.where(lane == 0, stat_sum, 0.0).astype(BF)

    mixed = dot_nt(attn[...], out_weight[...]).astype(BF)
    d_normed = dot_nt(d_qkv[...], weight[...]).astype(BF)
    for s, out in ((0, own_out), (1, sib_out)):
        out[0, 0, :, :FEAT] = mixed[s * CAP : (s + 1) * CAP]
        out[0, 1, :, :FEAT] = d_normed[s * CAP : (s + 1) * CAP]
        out[0, 0, :, FEAT:] = sums[s, 0]
        out[0, 1, :, FEAT:] = sums[s, 1]


def backward(place, qkv, d_mix, attn, probs, weight):
    whole = lambda *dims: pl.BlockSpec(dims, lambda i, p: (0,) * len(dims))
    piece = pl.BlockSpec((1, 2, CAP, FEAT + EXTRA), lambda i, p: (i, 0, 0, 0))
    piece_type = pltpu.HBM((NX, 2, CAP, FEAT + EXTRA), BF)
    return pl.pallas_call(
        backward_kernel,
        grid_spec=pltpu.PrefetchScalarGridSpec(
            num_scalar_prefetch=1,
            grid=(NX,),
            in_specs=[
                whole(2 * CAP, 6 * HD),
                whole(NX, 2 * CAP, FEAT),
                pl.BlockSpec((D, 2 * HD), lambda i, p: (0, 6 + p[2])),
                whole(2 * CAP, 2 * HD),
                whole(2, 2, CAP, CAP),
                pl.BlockSpec((FEAT, 6 * HD), lambda i, p: (chunk_of(i, p), p[2])),
                pl.BlockSpec((FEAT, 2 * HD), lambda i, p: (chunk_of(i, p), 6 + p[2])),
            ],
            out_specs=[piece, piece],
            scratch_shapes=[
                pltpu.VMEM((2 * CAP, 6 * HD), BF),
                pltpu.VMEM((2, 2, CAP, EXTRA), BF),
                pltpu.VMEM((2 * CAP, 2 * HD), BF),
            ],
        ),
        out_shape=[piece_type, piece_type],
        compiler_params=pltpu.CompilerParams(vmem_limit_bytes=VMEM_LIMIT),
        cost_estimate=pl.CostEstimate(
            flops=2 * 256 * 4096 * 1024, bytes_accessed=14 << 20, transcendentals=0
        ),
        name="backward",
    )(place, qkv, d_mix, weight, attn, probs, weight, weight)


def stack_kernel(*refs):
    out = refs[-1]
    for j, block in enumerate(refs[:-1]):
        out[j] = block[...]


def stack(*blocks):
    whole = pl.BlockSpec(memory_space=pltpu.VMEM)
    return pl.pallas_call(
        stack_kernel,
        in_specs=[whole] * len(blocks),
        out_specs=whole,
        out_shape=jax.ShapeDtypeStruct((len(blocks),) + blocks[0].shape, BF),
        name="stack",
    )(*blocks)


def prep_kernel(place, mine, other, gain, router, live, normed, d_mix, stats):
    lane = lax.broadcasted_iota(jnp.int32, (CAP, 128), 1)
    for s, source in ((0, mine), (1, other)):
        rows = pl.ds(s * CAP, CAP)
        square = jnp.zeros((CAP, 1), F32)
        logit = jnp.zeros((CAP, 1), F32)
        for k in range(NX):
            x_abs = lax.rem(place[0] + k, NX)
            wide = source[k, 0].astype(F32)
            square += jnp.sum(wide * wide, axis=1, keepdims=True)
            logit += jnp.sum(wide * router[x_abs], axis=1, keepdims=True)
        inv = lax.rsqrt(square / D + EPS)
        gate = jax.nn.sigmoid(logit)
        stats[rows, :] = jnp.where(lane == 0, gate, inv)
        gate_live = jnp.where(live[rows, :] > 0.0, gate, 0.0)
        for k in range(NX):
            x_abs = lax.rem(place[0] + k, NX)
            wide = source[k, 0].astype(F32)
            normed[x_abs, rows, :] = (wide * inv * gain[x_abs]).astype(BF)
            d_mix[x_abs, rows, :] = (gate_live * source[k, 1].astype(F32)).astype(BF)


def prep(place, mine, other, gain, router, live):
    whole = pl.BlockSpec(memory_space=pltpu.VMEM)
    return pl.pallas_call(
        prep_kernel,
        in_specs=[pl.BlockSpec(memory_space=pltpu.SMEM)] + [whole] * 5,
        out_specs=[whole] * 3,
        out_shape=[
            jax.ShapeDtypeStruct((NX, 2 * CAP, FEAT), BF),
            jax.ShapeDtypeStruct((NX, 2 * CAP, FEAT), BF),
            jax.ShapeDtypeStruct((2 * CAP, 128), F32),
        ],
        compiler_params=pltpu.CompilerParams(vmem_limit_bytes=24 * 1024 * 1024),
        name="prep",
    )(place, mine, other, gain, router, live)


def pack_kernel(w_query, w_key, w_value, w_out, out):
    for core in range(NC):
        cols = pl.ds(core * 2 * HD, 2 * HD)
        for i, w in enumerate((w_query, w_key, w_value)):
            out[:, pl.ds((3 * core + i) * 2 * HD, 2 * HD)] = w[:, cols]
        out[:, pl.ds((6 + core) * 2 * HD, 2 * HD)] = w_out[:, cols]


def pack(*weights):
    whole = pl.BlockSpec(memory_space=pltpu.VMEM)
    return pl.pallas_call(
        pack_kernel,
        in_specs=[whole] * 4,
        out_specs=whole,
        out_shape=pltpu.HBM((64, 16 * HD), BF),
        name="pack",
    )(*weights)


def finish_kernel(
    place, own, got, sent_1, sent_2, sent_3, part, stats, gain, router, slots, tokens,
    cotangent, block_out, token_grad, updated, d_rows,
):
    step = pl.program_id(0)

    @pl.when(step == 0)
    def _():
        def summed(kind, cols):
            total = own[0, kind, :, cols].astype(F32) + got[0, kind, :, cols].astype(F32)
            for block in (sent_1, sent_2, sent_3):
                total += block[kind, :, cols].astype(F32)
            return total

        extra = pl.ds(FEAT, EXTRA)
        gate, inv = stats[:, :1], stats[:, 1:2]
        d_logit = summed(0, extra)[:, :1] * (1.0 - gate)
        stat = summed(1, extra)[:, :1] / D
        for j in range(0, FEAT, 256):
            cols = pl.ds(j, 256)
            rows = part[0, :, cols].astype(F32)
            updated[:, cols] = (rows + gate * summed(0, cols)).astype(BF)
            value = summed(1, cols) * gain[0, :, cols] - rows * inv * stat
            value = part[1, :, cols].astype(F32) + inv * value + d_logit * router[0, :, cols]
            d_rows[:, cols] = value.astype(BF)

    height = tokens.shape[0]
    row = lax.broadcasted_iota(jnp.int32, (height, CAP), 0) + step * height
    hits = jnp.where(row == slots[...], 1.0, 0.0)
    hit = jnp.sum(hits, axis=1, keepdims=True) > 0.0
    hits = hits.astype(BF)
    block_out[...] = jnp.where(hit, dot_nn(hits, updated[...]).astype(BF), tokens[...])
    token_grad[...] = jnp.where(hit, dot_nn(hits, d_rows[...]).astype(BF), cotangent[...])


def finish(place, own, got, sent, part, stats, gain, router, slots, tokens, cotangent):
    whole = lambda *dims: pl.BlockSpec(dims, lambda i, p: (0,) * len(dims))
    local = pl.BlockSpec((1, 1, FEAT), lambda i, p: (p[0], 0, 0))
    rows = tokens.shape[0]
    tile = pl.BlockSpec((rows // 4, FEAT), lambda i, p: (i, 0))
    piece = whole(1, 2, CAP, FEAT + EXTRA)
    return pl.pallas_call(
        finish_kernel,
        grid_spec=pltpu.PrefetchScalarGridSpec(
            num_scalar_prefetch=1,
            grid=(4,),
            in_specs=[piece, piece]
            + [whole(2, CAP, FEAT + EXTRA)] * 3
            + [whole(2, CAP, FEAT), whole(CAP, 128), local, local, whole(1, CAP), tile, tile],
            out_specs=[tile, tile],
            scratch_shapes=[pltpu.VMEM((CAP, FEAT), BF)] * 2,
        ),
        out_shape=[
            pltpu.HBM((rows, FEAT), BF),
            pltpu.HBM((rows, FEAT), BF),
        ],
        compiler_params=pltpu.CompilerParams(vmem_limit_bytes=VMEM_LIMIT),
        cost_estimate=pl.CostEstimate(
            flops=4 * rows * FEAT * CAP, bytes_accessed=11 << 20, transcendentals=0
        ),
        name="finish",
    )(place, own, got, *sent, part, stats, gain, router, slots, tokens, cotangent)


def high(left, right, dims):
    return lax.dot_general(
        left,
        right,
        (dims, ((), ())),
        precision=lax.Precision.HIGHEST,
        preferred_element_type=F32,
    )


def add_kernel(*refs):
    out = refs[-1]
    for j in range(out.shape[0]):
        total = refs[0][j].astype(F32)
        for block in refs[1:-1]:
            total = total + block[j].astype(F32)
        out[j] = total.astype(BF)


def add_up(*blocks):
    whole = pl.BlockSpec(memory_space=pltpu.VMEM)
    return pl.pallas_call(
        add_kernel,
        in_specs=[whole] * len(blocks),
        out_specs=whole,
        out_shape=jax.ShapeDtypeStruct(blocks[0].shape, BF),
        compiler_params=pltpu.CompilerParams(vmem_limit_bytes=SMALL_LIMIT),
        name="add",
    )(*blocks)


def gram_kernel(parts, total_out, gram_out):
    total = parts[0].astype(F32)
    for k in range(1, NZ):
        total = total + parts[k].astype(F32)
    total_out[...] = total
    for h in range(2):
        block = total[h * HD : (h + 1) * HD]
        gram_out[h] = high(block, block, ((1,), (1,)))


def gram_of(parts):
    return pl.pallas_call(
        gram_kernel,
        out_shape=[
            jax.ShapeDtypeStruct((2 * HD, 128), F32),
            jax.ShapeDtypeStruct((2, HD, HD), F32),
        ],
        compiler_params=pltpu.CompilerParams(vmem_limit_bytes=SMALL_LIMIT),
        name="gram",
    )(parts)


def total_kernel(pieces, out):
    total = pieces[0]
    for k in range(1, NZ * NY):
        total = total + pieces[k]
    for k in range(NZ * NY):
        out[k] = total


def total_of(pieces):
    return pl.pallas_call(
        total_kernel,
        out_shape=jax.ShapeDtypeStruct(pieces.shape, F32),
        name="total",
    )(pieces)


def muon_kernel(gram_in, total, out):
    row = lax.broadcasted_iota(jnp.int32, (HD, HD), 0)
    col = lax.broadcasted_iota(jnp.int32, (HD, HD), 1)
    eye = jnp.where(row == col, 1.0, 0.0).astype(F32)
    nn = ((1,), (0,))
    for h in range(2):
        gram = gram_in[h]
        diag = jnp.sum(gram * eye, axis=1, keepdims=True)
        inv = 1.0 / (jnp.sqrt(jnp.sum(diag, axis=0, keepdims=True)) + 1e-07)
        gram = gram * inv * inv
        step = COEF_A * eye + COEF_B * gram + COEF_C * high(gram, gram, nn)
        gram = high(high(step, gram, nn), step, nn)
        last = COEF_A * eye + COEF_B * gram + COEF_C * high(gram, gram, nn)
        step = high(last, step, nn) * (inv * (0.2 * math.sqrt(D)))
        block = total[h * HD : (h + 1) * HD]
        out[:, h * HD : (h + 1) * HD] = high(block, step, ((0,), (1,)))


def muon(gram, total):
    return pl.pallas_call(
        muon_kernel,
        out_shape=jax.ShapeDtypeStruct((128, 2 * HD), F32),
        compiler_params=pltpu.CompilerParams(vmem_limit_bytes=SMALL_LIMIT),
        name="muon",
    )(gram, total)


def per_device(
    tokens, cotangent, w_query, w_key, w_value, w_out, gain, w_router, chosen, counts, doc_start
):
    dp = lax.axis_index("dp")
    x = lax.axis_index("mp")
    c = lax.rem(dp, NC)
    y = lax.rem(lax.div(dp, NC), NY)
    place = jnp.stack([x, y, c]).astype(jnp.int32)

    packed = pack(w_query, w_key, w_value, w_out.T)
    weight = lax.all_gather(packed, "dp", axis=0, tiled=True)

    picks = chosen[:, None] == jnp.arange(tokens.shape[0])[None, :]
    onehot = picks.astype(BF)
    live_own = jnp.arange(CAP) < counts[0]
    docs_own = jnp.sum(jnp.where(picks, doc_start[None, :], 0), axis=1)
    rows_part = dot_nn(onehot, tokens).astype(BF)
    grad_part = dot_nn(onehot, cotangent).astype(BF)
    meta_own = jnp.stack([chosen, docs_own, live_own.astype(jnp.int32)])
    meta = jnp.stack([meta_own, swap_core(meta_own)])
    position, docs = meta[:, 0], meta[:, 1]
    live = meta[:, 2] > 0

    part = jnp.stack([rows_part, grad_part])
    around = stack(part, *[move_x(part, k) for k in (3, 2, 1)])
    normed, d_mix, stats = prep(
        place,
        around,
        swap_core(around),
        gain.reshape(NX, 1, FEAT),
        w_router.reshape(NX, 1, FEAT),
        live.reshape(2 * CAP, 1).astype(F32),
    )
    allowed = (
        (position[:, None, :] <= position[:, :, None])
        & (docs[:, None, :] == docs[:, :, None])
        & live[:, None, :]
    )
    allowed = allowed | jnp.eye(CAP, dtype=bool)[None]
    mask = allowed.reshape(2 * CAP, CAP).astype(F32)

    qkv, attn, probs, grad_0, grad_1, grad_2, grad_3 = forward(
        place, normed, d_mix, weight, mask
    )
    moved = [move_y(grad_1, 1), move_y(grad_3, 3), move_y(grad_2, 2)]

    own, sibling = backward(place, qkv, d_mix, attn, probs, weight)
    sibling = after(sibling, *moved)
    got = swap_core(sibling)
    sums = [(own[k].astype(F32) + got[k].astype(F32)).astype(BF) for k in (1, 3, 2)]

    column = add_up(grad_0, *moved)
    sent = [move_x(v, k) for v, k in zip(sums, (1, 3, 2))]
    column = lax.all_to_all(column, "dp", 0, 0, tiled=True, axis_index_groups=GROUPS_Z)
    total, gram = gram_of(column)
    pieces = gram.reshape(NZ * NY, 8, 128)
    pieces = lax.all_to_all(pieces, "dp", 0, 0, tiled=True, axis_index_groups=GROUPS_ZY)
    pieces = total_of(pieces)
    pieces, *sent = lax.optimization_barrier((pieces, *sent))
    gram = lax.all_to_all(pieces, "dp", 0, 0, tiled=True, axis_index_groups=GROUPS_ZY)
    block_out, token_grad = finish(
        place,
        own,
        got,
        sent,
        part,
        stats,
        gain.reshape(NX, 1, FEAT),
        w_router.reshape(NX, 1, FEAT),
        jnp.where(live_own, chosen, -1)[None],
        tokens,
        cotangent,
    )
    gram, block_out, token_grad = lax.optimization_barrier((gram, block_out, token_grad))
    ortho = muon(gram.reshape(2, HD, HD), total).reshape(2, 64, 2 * HD)
    own_cols = lax.dynamic_index_in_dim(ortho, c, 0, keepdims=False)
    other_cols = swap_core(lax.dynamic_index_in_dim(ortho, 1 - c, 0, keepdims=False))
    muon_step = jnp.where(
        c == 0,
        jnp.concatenate([own_cols, other_cols], axis=1),
        jnp.concatenate([other_cols, own_cols], axis=1),
    ).T

    return (block_out, token_grad, muon_step)


def solution(mesh):
    placed = (
        P("dp", "mp"),
        P("dp", "mp"),
        P("dp", "mp"),
        P("dp", "mp"),
        P("dp", "mp"),
        P("mp", "dp"),
        P(),
        P(),
        P("dp"),
        P("dp"),
        P("dp"),
    )
    return jax.shard_map(
        per_device,
        mesh=mesh,
        in_specs=placed,
        out_specs=(P("dp", "mp"), P("dp", "mp"), P("mp", "dp")),
        check_vma=False,
    )
```

```python
import math

import jax
import jax.numpy as jnp
from jax import lax
from jax.experimental import pallas as pl
from jax.experimental.pallas import tpu as pltpu
from jax.sharding import PartitionSpec as P

D = 4096
HD = 128
CAP = 128
NZ, NY, NC, NX = 8, 4, 2, 4
FEAT = D // NX
EXTRA = 128
EPS = 1e-06
COEF_A = 3.4445
COEF_B = -4.775
COEF_C = 2.0315
BF = jnp.bfloat16
F32 = jnp.float32
VMEM_LIMIT = 60 * 1024 * 1024
SMALL_LIMIT = 16 * 1024 * 1024


def dp_index(z, y, c):
    return ((z % NZ) * NY + (y % NY)) * NC + c


def dp_perm(dz, dy, dc):
    return [
        (dp_index(z, y, c), dp_index(z + dz, y + dy, (c + dc) % NC))
        for z in range(NZ)
        for y in range(NY)
        for c in range(NC)
    ]


GROUPS_ZY = [[dp_index(z, y, c) for z in range(NZ) for y in range(NY)] for c in range(NC)]
GROUPS_Z = [[dp_index(z, y, c) for z in range(NZ)] for y in range(NY) for c in range(NC)]


def after(value, *others):
    return lax.optimization_barrier((value,) + others)[0]


def move_y(v, k):
    return lax.ppermute(v, "dp", dp_perm(0, k, 0))


def swap_core(v):
    return lax.ppermute(v, "dp", dp_perm(0, 0, 1))


def move_x(v, k):
    return lax.ppermute(v, "mp", [(i, (i + k) % NX) for i in range(NX)])


def dot_nn(left, right):
    return jnp.dot(left, right, preferred_element_type=F32)


def dot_nt(left, right):
    return lax.dot_general(
        left, right, (((1,), (1,)), ((), ())), preferred_element_type=F32
    )


def dot_tn(left, right):
    return lax.dot_general(
        left, right, (((0,), (0,)), ((), ())), preferred_element_type=F32
    )


def chunk_of(step, place):
    return lax.rem(place[0] + step, NX)


def forward_kernel(
    place, normed, d_mix, weight, mask, qkv_out, attn_out, probs_out, *rest
):
    grads, (rows_v, mix_v, weight_v, qkv_acc, held, in_sems, out_sems) = rest[:NY], rest[NY:]
    x, y = place[0], place[1]
    cols = pl.ds(pl.multiple_of(place[2] * 6 * HD, 6 * HD), 6 * HD)

    def copies(k):
        chunk = chunk_of(k, place)
        rows = pl.ds(pl.multiple_of(chunk * FEAT, FEAT), FEAT)
        return (
            pltpu.make_async_copy(weight.at[rows, cols], weight_v.at[k], in_sems.at[0, k]),
            pltpu.make_async_copy(normed.at[chunk], rows_v.at[k], in_sems.at[1, k]),
            pltpu.make_async_copy(d_mix.at[chunk], mix_v.at[k], in_sems.at[2, k]),
        )

    fetch = [copies(k) for k in range(NX)]
    for k in range(NX):
        fetch[k][0].start()
        fetch[k][1].start()
    for k in range(NX):
        fetch[k][2].start()
    for k in range(NX):
        fetch[k][0].wait()
        fetch[k][1].wait()
        part = dot_nn(rows_v[k], weight_v[k])
        if k == 0:
            qkv_acc[...] = part
        else:
            qkv_acc[...] += part

    qkv_out[...] = qkv_acc[...].astype(BF)
    for s in range(2):
        rows = pl.ds(s * CAP, CAP)
        for h in range(2):
            query = qkv_out[rows, pl.ds(h * HD, HD)]
            key = qkv_out[rows, pl.ds((2 + h) * HD, HD)]
            value = qkv_out[rows, pl.ds((4 + h) * HD, HD)]
            scores = dot_nt(query, key) * HD ** (-0.5)
            scores = jnp.where(mask[rows, :] > 0.0, scores, -1e30)
            expo = jnp.exp(scores - jnp.max(scores, axis=1, keepdims=True))
            probs = expo / jnp.sum(expo, axis=1, keepdims=True)
            probs_out[s, h] = probs
            attn_out[rows, pl.ds(h * HD, HD)] = dot_nn(probs.astype(BF), value).astype(BF)
    row = lax.broadcasted_iota(jnp.int32, (2 * CAP, 2 * CAP), 0)
    col = lax.broadcasted_iota(jnp.int32, (2 * CAP, 2 * CAP), 1)
    eye = jnp.where(row == col, 1.0, 0.0).astype(BF)
    attn_t = dot_tn(attn_out[...], eye).astype(BF)
    for k in range(NX):
        fetch[k][2].wait()
    sends = [pltpu.make_async_copy(held.at[k], grads[k], out_sems.at[k]) for k in range(NY)]
    for k in (2, 1, 3, 0):
        y_abs = lax.rem(y + k, NY)
        for i in range(NX):
            low = mix_v[i, :, pl.ds(pl.multiple_of(y_abs * 128, 128), 128)]
            high = mix_v[i, :, pl.ds(pl.multiple_of(512 + y_abs * 128, 128), 128)]
            res = dot_nn(attn_t, jnp.concatenate([low, high], axis=1)).astype(BF)
            x_abs = lax.rem(x + i, NX)
            held[k, 2 * x_abs] = res[:, :128]
            held[k, 2 * x_abs + 1] = res[:, 128:]
        sends[k].start()
    for k in range(NY):
        sends[k].wait()


def forward(place, normed, d_mix, weight, mask):
    whole = pl.BlockSpec(memory_space=pltpu.VMEM)
    outside = pl.BlockSpec(memory_space=pl.ANY)
    return pl.pallas_call(
        forward_kernel,
        in_specs=[pl.BlockSpec(memory_space=pltpu.SMEM)] + [outside] * 3 + [whole],
        out_specs=[whole] * 3 + [outside] * NY,
        scratch_shapes=[
            pltpu.VMEM((NX, 2 * CAP, FEAT), BF),
            pltpu.VMEM((NX, 2 * CAP, FEAT), BF),
            pltpu.VMEM((NX, FEAT, 6 * HD), BF),
            pltpu.VMEM((2 * CAP, 6 * HD), F32),
            pltpu.VMEM((NY, NZ, 2 * HD, 128), BF),
            pltpu.SemaphoreType.DMA((3, NX)),
            pltpu.SemaphoreType.DMA((NY,)),
        ],
        out_shape=[
            jax.ShapeDtypeStruct((2 * CAP, 6 * HD), BF),
            jax.ShapeDtypeStruct((2 * CAP, 2 * HD), BF),
            jax.ShapeDtypeStruct((2, 2, CAP, CAP), F32),
        ]
        + [pltpu.HBM((NZ, 2 * HD, 128), BF)] * NY,
        compiler_params=pltpu.CompilerParams(vmem_limit_bytes=VMEM_LIMIT),
        cost_estimate=pl.CostEstimate(
            flops=2 * 256 * 4096 * 1024, bytes_accessed=13 << 20, transcendentals=1 << 16
        ),
        name="forward",
    )(place, normed, d_mix, weight, mask)


def backward_kernel(
    place, qkv, d_mix, out_all, attn, probs_in, weight, out_weight,
    own_out, sib_out, d_qkv, sums, d_attn,
):
    step = pl.program_id(0)

    @pl.when(step == 0)
    def _():
        total = dot_nn(d_mix[0], out_all[:FEAT])
        for i in range(1, NX):
            total += dot_nn(d_mix[i], out_all[i * FEAT : (i + 1) * FEAT])
        d_attn[...] = total.astype(BF)
        lane = lax.broadcasted_iota(jnp.int32, (CAP, EXTRA), 1)
        for s in range(2):
            rows = pl.ds(s * CAP, CAP)
            gate_sum = jnp.zeros((CAP, 1), F32)
            stat_sum = jnp.zeros((CAP, 1), F32)
            for h in range(2):
                query = qkv[rows, pl.ds(h * HD, HD)]
                key = qkv[rows, pl.ds((2 + h) * HD, HD)]
                value = qkv[rows, pl.ds((4 + h) * HD, HD)]
                d_head = d_attn[rows, pl.ds(h * HD, HD)]
                probs = probs_in[s, h]
                d_probs = dot_nt(d_head, value)
                row_sum = jnp.sum(d_probs * probs, axis=1, keepdims=True)
                d_scores = (probs * (d_probs - row_sum) * HD ** (-0.5)).astype(BF)
                d_query = dot_nn(d_scores, key).astype(BF)
                d_key = dot_tn(d_scores, query).astype(BF)
                d_value = dot_tn(probs.astype(BF), d_head).astype(BF)
                d_qkv[rows, pl.ds(h * HD, HD)] = d_query
                d_qkv[rows, pl.ds((2 + h) * HD, HD)] = d_key
                d_qkv[rows, pl.ds((4 + h) * HD, HD)] = d_value
                out = attn[rows, pl.ds(h * HD, HD)]
                gate_sum += jnp.sum(out.astype(F32) * d_head.astype(F32), axis=1, keepdims=True)
                stat_sum += jnp.sum(
                    query.astype(F32) * d_query.astype(F32)
                    + key.astype(F32) * d_key.astype(F32)
                    + value.astype(F32) * d_value.astype(F32),
                    axis=1,
                    keepdims=True,
                )
            sums[s, 0] = jnp.where(lane == 0, gate_sum, 0.0).astype(BF)
            sums[s, 1] = jnp.where(lane == 0, stat_sum, 0.0).astype(BF)

    mixed = dot_nt(attn[...], out_weight[...]).astype(BF)
    d_normed = dot_nt(d_qkv[...], weight[...]).astype(BF)
    for s, out in ((0, own_out), (1, sib_out)):
        out[0, 0, :, :FEAT] = mixed[s * CAP : (s + 1) * CAP]
        out[0, 1, :, :FEAT] = d_normed[s * CAP : (s + 1) * CAP]
        out[0, 0, :, FEAT:] = sums[s, 0]
        out[0, 1, :, FEAT:] = sums[s, 1]


def backward(place, qkv, d_mix, attn, probs, weight):
    whole = lambda *dims: pl.BlockSpec(dims, lambda i, p: (0,) * len(dims))
    piece = pl.BlockSpec((1, 2, CAP, FEAT + EXTRA), lambda i, p: (i, 0, 0, 0))
    piece_type = pltpu.HBM((NX, 2, CAP, FEAT + EXTRA), BF)
    return pl.pallas_call(
        backward_kernel,
        grid_spec=pltpu.PrefetchScalarGridSpec(
            num_scalar_prefetch=1,
            grid=(NX,),
            in_specs=[
                whole(2 * CAP, 6 * HD),
                whole(NX, 2 * CAP, FEAT),
                pl.BlockSpec((D, 2 * HD), lambda i, p: (0, 6 + p[2])),
                whole(2 * CAP, 2 * HD),
                whole(2, 2, CAP, CAP),
                pl.BlockSpec((FEAT, 6 * HD), lambda i, p: (chunk_of(i, p), p[2])),
                pl.BlockSpec((FEAT, 2 * HD), lambda i, p: (chunk_of(i, p), 6 + p[2])),
            ],
            out_specs=[piece, piece],
            scratch_shapes=[
                pltpu.VMEM((2 * CAP, 6 * HD), BF),
                pltpu.VMEM((2, 2, CAP, EXTRA), BF),
                pltpu.VMEM((2 * CAP, 2 * HD), BF),
            ],
        ),
        out_shape=[piece_type, piece_type],
        compiler_params=pltpu.CompilerParams(vmem_limit_bytes=VMEM_LIMIT),
        cost_estimate=pl.CostEstimate(
            flops=2 * 256 * 4096 * 1024, bytes_accessed=14 << 20, transcendentals=0
        ),
        name="backward",
    )(place, qkv, d_mix, weight, attn, probs, weight, weight)


def stack_kernel(*refs):
    out = refs[-1]
    for j, block in enumerate(refs[:-1]):
        out[j] = block[...]


def stack(*blocks):
    whole = pl.BlockSpec(memory_space=pltpu.VMEM)
    return pl.pallas_call(
        stack_kernel,
        in_specs=[whole] * len(blocks),
        out_specs=whole,
        out_shape=jax.ShapeDtypeStruct((len(blocks),) + blocks[0].shape, BF),
        name="stack",
    )(*blocks)


def prep_kernel(place, mine, other, gain, router, live, normed, d_mix, stats):
    lane = lax.broadcasted_iota(jnp.int32, (CAP, 128), 1)
    for s, source in ((0, mine), (1, other)):
        rows = pl.ds(s * CAP, CAP)
        square = jnp.zeros((CAP, 1), F32)
        logit = jnp.zeros((CAP, 1), F32)
        for k in range(NX):
            x_abs = lax.rem(place[0] + k, NX)
            wide = source[k, 0].astype(F32)
            square += jnp.sum(wide * wide, axis=1, keepdims=True)
            logit += jnp.sum(wide * router[x_abs], axis=1, keepdims=True)
        inv = lax.rsqrt(square / D + EPS)
        gate = jax.nn.sigmoid(logit)
        stats[rows, :] = jnp.where(lane == 0, gate, inv)
        gate_live = jnp.where(live[rows, :] > 0.0, gate, 0.0)
        for k in range(NX):
            x_abs = lax.rem(place[0] + k, NX)
            wide = source[k, 0].astype(F32)
            normed[x_abs, rows, :] = (wide * inv * gain[x_abs]).astype(BF)
            d_mix[x_abs, rows, :] = (gate_live * source[k, 1].astype(F32)).astype(BF)


def prep(place, mine, other, gain, router, live):
    whole = pl.BlockSpec(memory_space=pltpu.VMEM)
    return pl.pallas_call(
        prep_kernel,
        in_specs=[pl.BlockSpec(memory_space=pltpu.SMEM)] + [whole] * 5,
        out_specs=[whole] * 3,
        out_shape=[
            jax.ShapeDtypeStruct((NX, 2 * CAP, FEAT), BF),
            jax.ShapeDtypeStruct((NX, 2 * CAP, FEAT), BF),
            jax.ShapeDtypeStruct((2 * CAP, 128), F32),
        ],
        compiler_params=pltpu.CompilerParams(vmem_limit_bytes=24 * 1024 * 1024),
        name="prep",
    )(place, mine, other, gain, router, live)


def pack_kernel(w_query, w_key, w_value, w_out, out, sems):
    moves = []
    for core in range(NC):
        cols = pl.ds(core * 2 * HD, 2 * HD)
        for i, w in enumerate((w_query, w_key, w_value, w_out)):
            block = 3 * core + i if i < 3 else 6 + core
            target = out.at[:, pl.ds(block * 2 * HD, 2 * HD)]
            moves.append(pltpu.make_async_copy(w.at[:, cols], target, sems.at[4 * core + i]))
    for move in moves:
        move.start()
    for move in moves:
        move.wait()


def pack(*weights):
    outside = pl.BlockSpec(memory_space=pl.ANY)
    return pl.pallas_call(
        pack_kernel,
        in_specs=[outside] * 4,
        out_specs=outside,
        out_shape=pltpu.HBM((64, 16 * HD), BF),
        scratch_shapes=[pltpu.SemaphoreType.DMA((8,))],
        compiler_params=pltpu.CompilerParams(vmem_limit_bytes=VMEM_LIMIT),
        name="pack",
    )(*weights)


def finish_kernel(
    place, own, got, sent_1, sent_2, sent_3, part, stats, gain, router, slots, tokens,
    cotangent, block_out, token_grad, updated, d_rows,
):
    step = pl.program_id(0)

    @pl.when(step == 0)
    def _():
        def summed(kind, cols):
            total = own[0, kind, :, cols].astype(F32) + got[0, kind, :, cols].astype(F32)
            for block in (sent_1, sent_2, sent_3):
                total += block[kind, :, cols].astype(F32)
            return total

        extra = pl.ds(FEAT, EXTRA)
        gate, inv = stats[:, :1], stats[:, 1:2]
        d_logit = summed(0, extra)[:, :1] * (1.0 - gate)
        stat = summed(1, extra)[:, :1] / D
        for j in range(0, FEAT, 256):
            cols = pl.ds(j, 256)
            rows = part[0, :, cols].astype(F32)
            updated[:, cols] = (rows + gate * summed(0, cols)).astype(BF)
            value = summed(1, cols) * gain[0, :, cols] - rows * inv * stat
            value = part[1, :, cols].astype(F32) + inv * value + d_logit * router[0, :, cols]
            d_rows[:, cols] = value.astype(BF)

    height = tokens.shape[0]
    row = lax.broadcasted_iota(jnp.int32, (height, CAP), 0) + step * height
    hits = jnp.where(row == slots[...], 1.0, 0.0)
    hit = jnp.sum(hits, axis=1, keepdims=True) > 0.0
    hits = hits.astype(BF)
    block_out[...] = jnp.where(hit, dot_nn(hits, updated[...]).astype(BF), tokens[...])
    token_grad[...] = jnp.where(hit, dot_nn(hits, d_rows[...]).astype(BF), cotangent[...])


def finish(place, own, got, sent, part, stats, gain, router, slots, tokens, cotangent):
    whole = lambda *dims: pl.BlockSpec(dims, lambda i, p: (0,) * len(dims))
    local = pl.BlockSpec((1, 1, FEAT), lambda i, p: (p[0], 0, 0))
    rows = tokens.shape[0]
    tile = pl.BlockSpec((rows // 4, FEAT), lambda i, p: (i, 0))
    piece = whole(1, 2, CAP, FEAT + EXTRA)
    return pl.pallas_call(
        finish_kernel,
        grid_spec=pltpu.PrefetchScalarGridSpec(
            num_scalar_prefetch=1,
            grid=(4,),
            in_specs=[piece, piece]
            + [whole(2, CAP, FEAT + EXTRA)] * 3
            + [whole(2, CAP, FEAT), whole(CAP, 128), local, local, whole(1, CAP), tile, tile],
            out_specs=[tile, tile],
            scratch_shapes=[pltpu.VMEM((CAP, FEAT), BF)] * 2,
        ),
        out_shape=[
            pltpu.HBM((rows, FEAT), BF),
            pltpu.HBM((rows, FEAT), BF),
        ],
        compiler_params=pltpu.CompilerParams(vmem_limit_bytes=VMEM_LIMIT),
        cost_estimate=pl.CostEstimate(
            flops=4 * rows * FEAT * CAP, bytes_accessed=11 << 20, transcendentals=0
        ),
        name="finish",
    )(place, own, got, *sent, part, stats, gain, router, slots, tokens, cotangent)


def high(left, right, dims):
    return lax.dot_general(
        left,
        right,
        (dims, ((), ())),
        precision=lax.Precision.HIGHEST,
        preferred_element_type=F32,
    )


def add_kernel(*refs):
    out = refs[-1]
    for j in range(out.shape[0]):
        total = refs[0][j].astype(F32)
        for block in refs[1:-1]:
            total = total + block[j].astype(F32)
        out[j] = total.astype(BF)


def add_up(*blocks):
    whole = pl.BlockSpec(memory_space=pltpu.VMEM)
    return pl.pallas_call(
        add_kernel,
        in_specs=[whole] * len(blocks),
        out_specs=whole,
        out_shape=jax.ShapeDtypeStruct(blocks[0].shape, BF),
        compiler_params=pltpu.CompilerParams(vmem_limit_bytes=SMALL_LIMIT),
        name="add",
    )(*blocks)


def gram_kernel(parts, total_out, gram_out):
    total = parts[0].astype(F32)
    for k in range(1, NZ):
        total = total + parts[k].astype(F32)
    total_out[...] = total
    for h in range(2):
        block = total[h * HD : (h + 1) * HD]
        gram_out[h] = high(block, block, ((1,), (1,)))


def gram_of(parts):
    return pl.pallas_call(
        gram_kernel,
        out_shape=[
            jax.ShapeDtypeStruct((2 * HD, 128), F32),
            jax.ShapeDtypeStruct((2, HD, HD), F32),
        ],
        compiler_params=pltpu.CompilerParams(vmem_limit_bytes=SMALL_LIMIT),
        name="gram",
    )(parts)


def total_kernel(pieces, out):
    total = pieces[0]
    for k in range(1, NZ * NY):
        total = total + pieces[k]
    for k in range(NZ * NY):
        out[k] = total


def total_of(pieces):
    return pl.pallas_call(
        total_kernel,
        out_shape=jax.ShapeDtypeStruct(pieces.shape, F32),
        name="total",
    )(pieces)


def muon_kernel(gram_in, total, out):
    row = lax.broadcasted_iota(jnp.int32, (HD, HD), 0)
    col = lax.broadcasted_iota(jnp.int32, (HD, HD), 1)
    eye = jnp.where(row == col, 1.0, 0.0).astype(F32)
    nn = ((1,), (0,))
    for h in range(2):
        gram = gram_in[h]
        diag = jnp.sum(gram * eye, axis=1, keepdims=True)
        inv = 1.0 / (jnp.sqrt(jnp.sum(diag, axis=0, keepdims=True)) + 1e-07)
        gram = gram * inv * inv
        step = COEF_A * eye + COEF_B * gram + COEF_C * high(gram, gram, nn)
        gram = high(high(step, gram, nn), step, nn)
        last = COEF_A * eye + COEF_B * gram + COEF_C * high(gram, gram, nn)
        step = high(last, step, nn) * (inv * (0.2 * math.sqrt(D)))
        block = total[h * HD : (h + 1) * HD]
        out[:, h * HD : (h + 1) * HD] = high(block, step, ((0,), (1,)))


def muon(gram, total):
    return pl.pallas_call(
        muon_kernel,
        out_shape=jax.ShapeDtypeStruct((128, 2 * HD), F32),
        compiler_params=pltpu.CompilerParams(vmem_limit_bytes=SMALL_LIMIT),
        name="muon",
    )(gram, total)


def per_device(
    tokens, cotangent, w_query, w_key, w_value, w_out, gain, w_router, chosen, counts, doc_start
):
    dp = lax.axis_index("dp")
    x = lax.axis_index("mp")
    c = lax.rem(dp, NC)
    y = lax.rem(lax.div(dp, NC), NY)
    place = jnp.stack([x, y, c]).astype(jnp.int32)

    packed = pack(w_query, w_key, w_value, w_out.T)
    weight = lax.all_gather(packed, "dp", axis=0, tiled=True)

    picks = chosen[:, None] == jnp.arange(tokens.shape[0])[None, :]
    onehot = picks.astype(BF)
    live_own = jnp.arange(CAP) < counts[0]
    docs_own = jnp.sum(jnp.where(picks, doc_start[None, :], 0), axis=1)
    rows_part = dot_nn(onehot, tokens).astype(BF)
    grad_part = dot_nn(onehot, cotangent).astype(BF)
    meta_own = jnp.stack([chosen, docs_own, live_own.astype(jnp.int32)])
    meta = jnp.stack([meta_own, swap_core(meta_own)])
    position, docs = meta[:, 0], meta[:, 1]
    live = meta[:, 2] > 0

    part = jnp.stack([rows_part, grad_part])
    around = stack(part, *[move_x(part, k) for k in (3, 2, 1)])
    normed, d_mix, stats = prep(
        place,
        around,
        swap_core(around),
        gain.reshape(NX, 1, FEAT),
        w_router.reshape(NX, 1, FEAT),
        live.reshape(2 * CAP, 1).astype(F32),
    )
    allowed = (
        (position[:, None, :] <= position[:, :, None])
        & (docs[:, None, :] == docs[:, :, None])
        & live[:, None, :]
    )
    allowed = allowed | jnp.eye(CAP, dtype=bool)[None]
    mask = allowed.reshape(2 * CAP, CAP).astype(F32)

    qkv, attn, probs, grad_0, grad_1, grad_2, grad_3 = forward(
        place, normed, d_mix, weight, mask
    )
    moved = [move_y(grad_1, 1), move_y(grad_3, 3), move_y(grad_2, 2)]

    own, sibling = backward(place, qkv, d_mix, attn, probs, weight)
    sibling = after(sibling, *moved)
    got = swap_core(sibling)
    sums = [(own[k].astype(F32) + got[k].astype(F32)).astype(BF) for k in (1, 3, 2)]

    column = add_up(grad_0, *moved)
    sent = [move_x(v, k) for v, k in zip(sums, (1, 3, 2))]
    column = lax.all_to_all(column, "dp", 0, 0, tiled=True, axis_index_groups=GROUPS_Z)
    total, gram = gram_of(column)
    pieces = gram.reshape(NZ * NY, 8, 128)
    pieces = lax.all_to_all(pieces, "dp", 0, 0, tiled=True, axis_index_groups=GROUPS_ZY)
    pieces = total_of(pieces)
    pieces, *sent = lax.optimization_barrier((pieces, *sent))
    gram = lax.all_to_all(pieces, "dp", 0, 0, tiled=True, axis_index_groups=GROUPS_ZY)
    block_out, token_grad = finish(
        place,
        own,
        got,
        sent,
        part,
        stats,
        gain.reshape(NX, 1, FEAT),
        w_router.reshape(NX, 1, FEAT),
        jnp.where(live_own, chosen, -1)[None],
        tokens,
        cotangent,
    )
    gram, block_out, token_grad = lax.optimization_barrier((gram, block_out, token_grad))
    ortho = muon(gram.reshape(2, HD, HD), total).reshape(2, 64, 2 * HD)
    own_cols = lax.dynamic_index_in_dim(ortho, c, 0, keepdims=False)
    other_cols = swap_core(lax.dynamic_index_in_dim(ortho, 1 - c, 0, keepdims=False))
    muon_step = jnp.where(
        c == 0,
        jnp.concatenate([own_cols, other_cols], axis=1),
        jnp.concatenate([other_cols, own_cols], axis=1),
    ).T

    return (block_out, token_grad, muon_step)


def solution(mesh):
    placed = (
        P("dp", "mp"),
        P("dp", "mp"),
        P("dp", "mp"),
        P("dp", "mp"),
        P("dp", "mp"),
        P("mp", "dp"),
        P(),
        P(),
        P("dp"),
        P("dp"),
        P("dp"),
    )
    return jax.shard_map(
        per_device,
        mesh=mesh,
        in_specs=placed,
        out_specs=(P("dp", "mp"), P("dp", "mp"), P("mp", "dp")),
        check_vma=False,
    )
```
